512 devices in a mesh: src: 16 (over z_lo, core), dst: 32 (over z_hi, x, y).
Axes of the slice: x: 4, y: 4, z: 16 (z_hi: 2, z_lo: 8; z = z_hi * 8 + z_lo), core: 2. Of those that a mesh axis runs over, the one named last changes fastest.
Arguments:
- src_emb: float32 [16, 32, 384, 256], P('src', 'dst'), may hold values from -3 to 3
- src_state: float32 [16, 32, 384], P('src', 'dst'), may hold values from 0.01 to 1
- dst_emb: float32 [16, 32, 1024, 256], P('src', 'dst'), may hold values from -3 to 3
- dst_state: float32 [16, 32, 1024], P('src', 'dst'), may hold values from 0.01 to 1
- src_ids: int32 [16, 32, 256], P('src', 'dst'), may hold values from 0 to 6143
- dst_ids: int32 [16, 32, 256], P('src', 'dst'), may hold values from 0 to 1023
- neg_ids: int32 [16, 32, 1024], P('src', 'dst'), may hold values from 0 to 1023
- counts: int32 [16, 32], P('src', 'dst'), may hold values from 64 to 256, as said below
Outputs:
- src_new: float32 [16, 32, 384, 256], P('src', 'dst')
- src_state_new: float32 [16, 32, 384], P('src', 'dst')
- dst_new: float32 [16, 32, 1024, 256], P('src', 'dst')
- dst_state_new: float32 [16, 32, 1024], P('src', 'dst')
- edge_loss: float32 [16, 32, 256], P('src', 'dst')
The draws below stay inside these ranges and needn't reach their ends.
Inputs may be any that keep to these rules, and one draw needn't show every extreme that they name: `counts`: each block has 64 to 256 live edges, and some block has exactly 256.
All inputs are finite; a program needn't handle non-finite values.
Results may differ from the reference program's by a relative error of at most 0.0003.
Values sent between devices are 32-bit elements; how exact they have to be, the bound alone decides.
No kernel may reach another device: no remote copies, remote signals or barrier semaphores. Data moves between devices by JAX's collectives and lax.ppermute only.
A program may use at most 64 MiB of HBM per device.

```python
import math
import jax
import jax.numpy as jnp
from jax import lax

D = 256
SR = 384
DR = 1024
EDGES = 256
NEG = 1024
SRC_PART = 6144
N_SRC = 16
N_DST = 32


def draw_src_emb(key, part):
    key = jax.random.fold_in(key, 11)
    noise_key = jax.random.fold_in(key, 0)
    noise = jax.random.normal(noise_key, (N_SRC, N_DST, SR, D), jnp.float32)
    return 0.45 * jnp.clip(noise, -6.6, 6.6)


def draw_dst_emb(key, part):
    key = jax.random.fold_in(key, 12)
    noise_key = jax.random.fold_in(key, 0)
    noise = jax.random.normal(noise_key, (N_SRC, N_DST, DR, D), jnp.float32)
    return 0.45 * jnp.clip(noise, -6.6, 6.6)


def draw_counts(key, part):
    key = jax.random.fold_in(key, 13)
    value_key, spot_key = jax.random.split(key)
    values = jax.random.randint(value_key, (N_SRC, N_DST), EDGES // 4, EDGES + 1)
    spot = jax.random.randint(spot_key, (), 0, N_SRC * N_DST)
    places = jnp.arange(N_SRC * N_DST, dtype=jnp.int32).reshape(N_SRC, N_DST)
    return jnp.where(places == spot, EDGES, values).astype(jnp.int32)


def plant(result, own_key, least, high):
    longest = result.shape.index(max(result.shape))
    spots = []
    for shift in (0, 1):
        where = [jax.random.randint(jax.random.fold_in(own_key, axis), (), 0, length) for axis, length in enumerate(result.shape)]
        where[longest] = (where[longest] + shift) % result.shape[longest]
        spots.append(tuple(where))
    return result.at[spots[0]].set(least).at[spots[1]].set(high)


def steps_of(key, extent, shards, low, top_value):
    def one(position, shards_of):
        draws = jax.random.uniform(jax.random.fold_in(jax.random.fold_in(key, 6), position), (shards_of,), jnp.float32, low / len(shards), top_value / len(shards))
        return jnp.repeat(jnp.exp(draws), extent[position] // shards_of).reshape((-1,) + (1,) * (len(extent) - position - 1))

    gain = one(*shards[0])
    for cut in shards[1:]:
        gain = gain * one(*cut)
    return gain


def setup_inputs(seed: int = 0) -> dict:
    key_of = jax.random.split(jax.random.key(seed), 9)
    return {
        "src_emb": draw_src_emb(jax.random.fold_in(key_of[8], 71), 0),
        "src_state": jnp.clip(jnp.exp(math.log(1.0) - 4.6051702 * jax.random.uniform(key_of[1], (N_SRC, N_DST, SR), jnp.float32) ** steps_of(key_of[1], (N_SRC, N_DST, SR), ((0, 16), (1, 32)), -0.2, 0.2)), 0.01, 1.0),
        "dst_emb": draw_dst_emb(jax.random.fold_in(key_of[8], 71), 0),
        "dst_state": jnp.clip(jnp.exp(math.log(1.0) - 4.6051702 * jax.random.uniform(key_of[3], (N_SRC, N_DST, DR), jnp.float32) ** steps_of(key_of[3], (N_SRC, N_DST, DR), ((0, 16), (1, 32)), -0.2, 0.2)), 0.01, 1.0),
        "src_ids": plant(jax.random.randint(key_of[4], (N_SRC, N_DST, EDGES), 0, SRC_PART), jax.random.fold_in(key_of[4], 1), 0, SRC_PART - 1).astype(jnp.int32),
        "dst_ids": plant(jax.random.randint(key_of[5], (N_SRC, N_DST, EDGES), 0, DR), jax.random.fold_in(key_of[5], 1), 0, DR - 1).astype(jnp.int32),
        "neg_ids": plant(jax.random.randint(key_of[6], (N_SRC, N_DST, NEG), 0, DR), jax.random.fold_in(key_of[6], 1), 0, DR - 1).astype(jnp.int32),
        "counts": draw_counts(jax.random.fold_in(key_of[8], 71), 0),
    }


def adagrad(emb, state, grad):
    state_new = state + lax.optimization_barrier(jnp.mean(grad * grad, axis=-1))
    emb_new = emb - 0.1 * grad / (jnp.sqrt(state_new)[..., None] + 1e-10)
    return (emb_new, state_new)

def reference(src_emb, src_state, dst_emb, dst_state, src_ids, dst_ids, neg_ids, counts):
    highest = lax.Precision.HIGHEST
    partitions = jnp.transpose(src_emb, (1, 0, 2, 3)).reshape(N_DST, N_SRC * SR, D)
    table = jnp.roll(dst_emb, 1, axis=1)
    table_state = jnp.roll(dst_state, 1, axis=1)

    def bucket(index):
        row_block = index // N_DST
        col_block = index % N_DST
        part_rows = partitions[col_block]
        slice_rows = table[row_block, col_block]
        sources = part_rows[src_ids[row_block, col_block]]
        targets = slice_rows[dst_ids[row_block, col_block]]
        negatives = slice_rows[neg_ids[row_block, col_block]]
        positive = lax.optimization_barrier(jnp.sum(sources * targets, axis=1))
        scores = jnp.dot(sources, negatives.T, precision=highest)
        live = (jnp.arange(EDGES, dtype=jnp.int32) < counts[row_block, col_block]).astype(jnp.float32)
        top = jnp.maximum(lax.optimization_barrier(jnp.max(scores, axis=1)), positive)
        total = jnp.exp(positive - top) + lax.optimization_barrier(jnp.sum(jnp.exp(scores - top[:, None]), axis=1))
        logsum = top + jnp.log(total)
        loss = live * (logsum - positive)
        dpos = live * (jnp.exp(positive - logsum) - 1.0)
        dneg = live[:, None] * jnp.exp(scores - logsum[:, None])
        source_grad = dpos[:, None] * targets + jnp.dot(dneg, negatives, precision=highest)
        target_grad = dpos[:, None] * sources
        negative_grad = jnp.dot(dneg.T, sources, precision=highest)
        dest_grad = jnp.zeros((DR, D), jnp.float32)
        dest_grad = dest_grad.at[dst_ids[row_block, col_block]].add(target_grad)
        dest_grad = dest_grad.at[neg_ids[row_block, col_block]].add(negative_grad)
        return (loss, source_grad, dest_grad)
    indices = jnp.arange(N_SRC * N_DST, dtype=jnp.int32)
    losses, source_grads, dest_grads = lax.map(bucket, indices)
    owners = (indices % N_DST)[:, None] * (N_SRC * SR) + src_ids.reshape(N_SRC * N_DST, EDGES)
    grad_rows = jax.ops.segment_sum(source_grads.reshape(-1, D), owners.reshape(-1), num_segments=N_DST * N_SRC * SR)
    grad_rows = jnp.transpose(grad_rows.reshape(N_DST, N_SRC, SR, D), (1, 0, 2, 3))
    src_new, src_state_new = adagrad(src_emb, src_state, grad_rows)
    dst_new, dst_state_new = adagrad(table, table_state, dest_grads.reshape(N_SRC, N_DST, DR, D))
    edge_loss = losses.reshape(N_SRC, N_DST, EDGES)
    return (src_new, src_state_new, dst_new, dst_state_new, edge_loss)
```

```python
import functools

import jax
import jax.numpy as jnp
from jax import lax
from jax.experimental import pallas as pl
from jax.experimental.pallas import tpu as pltpu
from jax.sharding import PartitionSpec as P

SLOTS = 40
F32 = jnp.float32
BF16 = jnp.bfloat16
VMEM = pl.BlockSpec(memory_space=pltpu.VMEM)
SMEM = pl.BlockSpec(memory_space=pltpu.SMEM)
ROWS = (((1,), (0,)), ((), ()))
LANES = (((1,), (1,)), ((), ()))
FIRST = (((0,), (0,)), ((), ()))


def mxu(left, right, dims=ROWS):
    return lax.dot_general(left, right, dims, preferred_element_type=F32)


def parts_of(value, count):
    parts = []
    for _ in range(count - 1):
        part = value.astype(BF16)
        parts.append(part)
        value = value - part.astype(F32)
    parts.append(value.astype(BF16))
    return parts


def pick(onehot, parts, dims=ROWS):
    total = mxu(onehot, parts[-1], dims)
    for part in parts[-2::-1]:
        total = total + mxu(onehot, part, dims)
    return total


def product(left, right, dims=ROWS):
    total = mxu(left[0], right[1], dims) + mxu(left[1], right[0], dims)
    if len(left) > 2:
        small = mxu(left[0], right[2], dims) + mxu(left[2], right[0], dims)
        total = (small + mxu(left[1], right[1], dims)) + total
    return total + mxu(left[0], right[0], dims)


def flag(condition):
    return jnp.where(condition, 1.0, 0.0).astype(F32)


def to_column(row):
    size = row.shape[1]
    down = lax.broadcasted_iota(jnp.int32, (size, size), 0)
    across = lax.broadcasted_iota(jnp.int32, (size, size), 1)
    return jnp.sum(jnp.where(down == across, row, 0.0), axis=1, keepdims=True)


def pack_rows_kernel(own, slots, first_ref, ids_ref, rows_ref, send_ref, local_ref):
    devices, edges = ids_ref.shape
    local = ids_ref[...] - first_ref[0]
    owned = flag((local >= 0) & (local < own))
    down = lax.broadcasted_iota(jnp.int32, (edges, edges), 0)
    across = lax.broadcasted_iota(jnp.int32, (edges, edges), 1)
    rank = mxu(owned.astype(BF16), flag(down < across).astype(BF16))
    rank = jnp.where(owned > 0.0, rank, -1.0)
    mark = local.astype(F32) + 1.0
    slot = lax.broadcasted_iota(jnp.int32, (slots, edges), 0).astype(F32)
    columns = []
    for device in range(devices):
        chosen = jnp.where(rank[device : device + 1] == slot, mark[device : device + 1], 0.0)
        columns.append(jnp.sum(chosen, axis=1, keepdims=True))
    column = jnp.concatenate(columns, axis=0) - 1.0
    local_ref[...] = column
    across = lax.broadcasted_iota(jnp.int32, (devices * slots, own), 1).astype(F32)
    hot = flag(across == column).astype(BF16)
    send_ref[...] = pick(hot, parts_of(rows_ref[...], 3))


def pack_rows(first, ids, rows, slots):
    devices = ids.shape[0]
    own, width = rows.shape
    return pl.pallas_call(
        functools.partial(pack_rows_kernel, own, slots),
        out_shape=(
            jax.ShapeDtypeStruct((devices * slots, width), F32),
            jax.ShapeDtypeStruct((devices * slots, 1), F32),
        ),
        in_specs=[SMEM, VMEM, VMEM],
        out_specs=(VMEM, VMEM),
        compiler_params=pltpu.CompilerParams(vmem_limit_bytes=40 << 20),
        name="pack_rows",
    )(first, ids, rows)


def edge_kernel(
    devices, own, slots, count_ref, ids_ref, dest_ref, negative_ref, got_ref, table_ref,
    loss_ref, back_ref, source_ref, weight_ref,
):
    edges = ids_ref.shape[1]
    height = table_ref.shape[0]
    ids = ids_ref[...]
    owner = jnp.zeros(ids.shape, F32)
    for device in range(1, devices):
        owner = owner + flag(ids >= device * own)
    down = lax.broadcasted_iota(jnp.int32, (edges, edges), 0)
    across = lax.broadcasted_iota(jnp.int32, (edges, edges), 1)
    before = flag((to_column(owner) == owner) & (down < across))
    rank = jnp.sum(before, axis=0, keepdims=True)
    place = jnp.where(rank < slots, owner * slots + rank, -1.0)
    place_column = to_column(place)
    across = lax.broadcasted_iota(jnp.int32, (edges, devices * slots), 1).astype(F32)
    source = pick(flag(across == place_column).astype(BF16), parts_of(got_ref[...], 3))
    source_ref[...] = source

    table = parts_of(table_ref[...], 3)
    scores = product(parts_of(source, 3), table, LANES)

    negative = negative_ref[...]
    low = 128
    high = height // low
    row = lax.broadcasted_iota(jnp.int32, (high, negative.shape[1]), 0)
    hot_high = flag(row == lax.shift_right_logical(negative, 7)).astype(BF16)
    row = lax.broadcasted_iota(jnp.int32, (low, negative.shape[1]), 0)
    hot_low = flag(row == (negative & (low - 1))).astype(BF16)
    grid = mxu(hot_high, hot_low, LANES)
    times = jnp.concatenate([grid[i : i + 1] for i in range(high)], axis=1)

    dest = to_column(dest_ref[...].astype(F32))
    across = lax.broadcasted_iota(jnp.int32, (edges, height), 1).astype(F32)
    hot = across == dest
    positive = jnp.sum(jnp.where(hot, scores, 0.0), axis=1, keepdims=True)
    seen = times > 0.0
    top = jnp.max(jnp.where(seen, scores, -jnp.inf), axis=1, keepdims=True)
    top = jnp.maximum(top, positive)
    power = jnp.where(seen, jnp.exp(scores - top), 0.0) * times
    power_positive = jnp.exp(positive - top)
    total = power_positive + jnp.sum(power, axis=1, keepdims=True)
    logsum = top + jnp.log(total)
    edge = lax.broadcasted_iota(jnp.int32, (edges, 1), 0)
    live = flag(edge < count_ref[0, 0])
    loss = live * (logsum - positive)
    loss_ref[...] = jnp.transpose(jnp.broadcast_to(loss, (edges, 128)))[0:1]
    scale = live / total
    dpos = live * (jnp.exp(positive - logsum) - 1.0)
    weight = power * scale + jnp.where(hot, dpos, 0.0)
    weight_ref[...] = weight

    grad = product(parts_of(weight, 2), table)
    down = lax.broadcasted_iota(jnp.int32, (devices * slots, edges), 0).astype(F32)
    back_ref[...] = pick(flag(down == place).astype(BF16), parts_of(grad, 3))


def edge_step(count, ids, dest, negative, got, table, devices, own):
    slots = got.shape[0] // devices
    edges = ids.shape[1]
    height, width = table.shape
    return pl.pallas_call(
        functools.partial(edge_kernel, devices, own, slots),
        out_shape=(
            jax.ShapeDtypeStruct((1, edges), F32),
            jax.ShapeDtypeStruct(got.shape, F32),
            jax.ShapeDtypeStruct((edges, width), F32),
            jax.ShapeDtypeStruct((edges, height), F32),
        ),
        in_specs=[SMEM] + [VMEM] * 5,
        out_specs=(VMEM,) * 4,
        compiler_params=pltpu.CompilerParams(vmem_limit_bytes=48 << 20),
        name="edge_step",
    )(count, ids, dest, negative, got, table)


def row_of(column):
    return jnp.transpose(jnp.broadcast_to(column, (column.shape[0], 128)))[0:1]


def column_of(row):
    return jnp.transpose(jnp.broadcast_to(row, (128, row.shape[1])))[:, 0:1]


def adagrad_rows(emb, state, grad):
    state_new = column_of(state) + jnp.mean(grad * grad, axis=1, keepdims=True)
    emb_new = emb - grad * (0.1 / (jnp.sqrt(state_new) + 1e-10))
    return emb_new, row_of(state_new)


def table_kernel(weight_ref, source_ref, table_ref, state_ref, new_ref, state_new_ref):
    grad = product(parts_of(weight_ref[...], 2), parts_of(source_ref[...], 2), FIRST)
    new_ref[...], state_new_ref[...] = adagrad_rows(table_ref[...], state_ref[...], grad)


def table_step(weight, source, table, state):
    return pl.pallas_call(
        table_kernel,
        out_shape=(
            jax.ShapeDtypeStruct(table.shape, F32),
            jax.ShapeDtypeStruct(state.shape, F32),
        ),
        in_specs=[VMEM] * 4,
        out_specs=(VMEM, VMEM),
        compiler_params=pltpu.CompilerParams(vmem_limit_bytes=48 << 20),
        name="table_step",
    )(weight, source, table, state)


def source_kernel(local_ref, back_ref, rows_ref, state_ref, new_ref, state_new_ref):
    own = rows_ref.shape[0]
    across = lax.broadcasted_iota(jnp.int32, (local_ref.shape[0], own), 1).astype(F32)
    hot = flag(across == local_ref[...]).astype(BF16)
    grad = pick(hot, parts_of(back_ref[...], 3), FIRST)
    new_ref[...], state_new_ref[...] = adagrad_rows(rows_ref[...], state_ref[...], grad)


def source_step(local, back, rows, state):
    return pl.pallas_call(
        source_kernel,
        out_shape=(
            jax.ShapeDtypeStruct(rows.shape, F32),
            jax.ShapeDtypeStruct(state.shape, F32),
        ),
        in_specs=[VMEM] * 4,
        out_specs=(VMEM, VMEM),
        compiler_params=pltpu.CompilerParams(vmem_limit_bytes=40 << 20),
        name="source_step",
    )(local, back, rows, state)


def exact(left, right, dims=ROWS):
    return lax.dot_general(left, right, dims, precision=lax.Precision.HIGHEST, preferred_element_type=F32)


def adagrad(emb, state, grad):
    state_new = state + jnp.mean(grad * grad, axis=-1)
    emb_new = emb - 0.1 * grad / (jnp.sqrt(state_new)[:, None] + 1e-10)
    return emb_new, state_new


def whole_step(rows, rows_state, table, table_state, ids, all_ids, dest, negative, count, first):
    piece = lax.all_gather(rows, "src", axis=0, tiled=True)
    columns = jnp.arange(piece.shape[0], dtype=jnp.int32)
    sources = exact((ids[:, None] == columns[None, :]).astype(F32), piece)
    index = jnp.arange(table.shape[0], dtype=jnp.int32)
    hot_dest = (dest[:, None] == index[None, :]).astype(F32)
    hot_negative = (negative[:, None] == index[None, :]).astype(F32)
    targets = exact(hot_dest, table)
    negatives = exact(hot_negative, table)
    positive = jnp.sum(sources * targets, axis=1)
    scores = exact(sources, negatives, LANES)
    live = (jnp.arange(ids.shape[0], dtype=jnp.int32) < count).astype(F32)
    top = jnp.maximum(jnp.max(scores, axis=1), positive)
    total = jnp.exp(positive - top) + jnp.sum(jnp.exp(scores - top[:, None]), axis=1)
    logsum = top + jnp.log(total)
    loss = live * (logsum - positive)
    dpos = live * (jnp.exp(positive - logsum) - 1.0)
    dneg = live[:, None] * jnp.exp(scores - logsum[:, None])
    source_grad = dpos[:, None] * targets + exact(dneg, negatives)
    dest_grad = exact(hot_dest, dpos[:, None] * sources, FIRST)
    dest_grad = dest_grad + exact(hot_negative, exact(dneg, sources, FIRST), FIRST)
    grad_piece = lax.all_gather(source_grad, "src", axis=0, tiled=True)
    own_index = first + jnp.arange(rows.shape[0], dtype=jnp.int32)
    onehot = (all_ids.reshape(-1)[:, None] == own_index[None, :]).astype(F32)
    own_grad = exact(onehot, grad_piece, FIRST)
    new, new_state = adagrad(rows, rows_state, own_grad)
    table_new, table_state_new = adagrad(table, table_state, dest_grad)
    return new, new_state, table_new, table_state_new, loss


def on_device(src_emb, src_state, dst_emb, dst_state, src_ids, dst_ids, neg_ids, counts):
    devices = lax.axis_size("src")
    behind = lax.axis_size("dst")
    pairs = [(source, (source + 1) % behind) for source in range(behind)]
    rows, rows_state = src_emb[0, 0], src_state[0, 0]
    own, width = rows.shape
    ids = src_ids[0, 0]
    first = lax.axis_index("src") * own
    all_ids = lax.all_gather(ids, "src", axis=0, tiled=False)
    table = lax.ppermute(dst_emb[0, 0], "dst", pairs)
    table_state = lax.ppermute(dst_state[0, 0], "dst", pairs)

    owner = lax.broadcasted_iota(jnp.int32, (1, devices, 1), 1)
    used = jnp.sum((all_ids[:, None, :] // own == owner).astype(F32), axis=2)
    over = jnp.max(used) > SLOTS

    send, local = pack_rows(first.reshape(1), all_ids, rows, SLOTS)
    got = lax.all_to_all(send, "src", 0, 0, tiled=True)
    loss, back, source, weight = edge_step(
        counts, src_ids[0], dst_ids[0], neg_ids[0], got, table, devices, own
    )
    back = lax.all_to_all(back, "src", 0, 0, tiled=True)
    dst_new, dst_state_new = table_step(weight, source, table, table_state[None])
    src_new, src_state_new = source_step(local, back, rows, rows_state[None])

    def again(carry):
        found = whole_step(
            rows, rows_state, table, table_state, ids, all_ids, dst_ids[0, 0], neg_ids[0, 0], counts[0, 0], first
        )
        return (jnp.bool_(False),) + found

    fast = (over, src_new, src_state_new[0], dst_new, dst_state_new[0], loss[0])
    done = lax.while_loop(lambda carry: carry[0], again, fast)
    return tuple(value[None, None] for value in done[1:])


def solution(mesh):
    spec = lambda rank: P("src", "dst", *([None] * (rank - 2)))
    return jax.shard_map(
        on_device,
        mesh=mesh,
        in_specs=tuple(spec(rank) for rank in (4, 3, 4, 3, 3, 3, 3, 2)),
        out_specs=tuple(spec(rank) for rank in (4, 3, 4, 3, 3)),
        check_vma=False,
    )
```

```python
import functools
import math

import jax
import jax.numpy as jnp
from jax import lax
from jax.experimental import pallas as pl
from jax.experimental.pallas import tpu as pltpu
from jax.sharding import Mesh, PartitionSpec as P

SLOTS = 40
LEAVE = ((-1, -1), (-1, 0), (0, -1), (-1, -2), (-2, -1))
LAND = ((0, 0), (-1, 0), (0, -1), (0, 1), (1, 0))
F32 = jnp.float32
BF16 = jnp.bfloat16
VMEM = pl.BlockSpec(memory_space=pltpu.VMEM)
SMEM = pl.BlockSpec(memory_space=pltpu.SMEM)
ROWS = (((1,), (0,)), ((), ()))
LANES = (((1,), (1,)), ((), ()))
FIRST = (((0,), (0,)), ((), ()))


def mxu(left, right, dims=ROWS):
    return lax.dot_general(left, right, dims, preferred_element_type=F32)


def parts_of(value, count):
    parts = []
    for _ in range(count - 1):
        part = value.astype(BF16)
        parts.append(part)
        value = value - part.astype(F32)
    parts.append(value.astype(BF16))
    return parts


def pick(onehot, parts, dims=ROWS):
    total = mxu(onehot, parts[-1], dims)
    for part in parts[-2::-1]:
        total = total + mxu(onehot, part, dims)
    return total


def product(left, right, dims=ROWS):
    total = mxu(left[0], right[1], dims) + mxu(left[1], right[0], dims)
    if len(left) > 2:
        small = mxu(left[0], right[2], dims) + mxu(left[2], right[0], dims)
        total = (small + mxu(left[1], right[1], dims)) + total
    return total + mxu(left[0], right[0], dims)


def flag(condition):
    return jnp.where(condition, 1.0, 0.0).astype(F32)


def to_column(row):
    size = row.shape[1]
    down = lax.broadcasted_iota(jnp.int32, (size, size), 0)
    across = lax.broadcasted_iota(jnp.int32, (size, size), 1)
    return jnp.sum(jnp.where(down == across, row, 0.0), axis=1, keepdims=True)


def pack_rows_kernel(own, slots, first_ref, ids_ref, rows_ref, send_ref, local_ref):
    devices, edges = ids_ref.shape
    local = ids_ref[...] - first_ref[0]
    owned = flag((local >= 0) & (local < own))
    down = lax.broadcasted_iota(jnp.int32, (edges, edges), 0)
    across = lax.broadcasted_iota(jnp.int32, (edges, edges), 1)
    rank = mxu(owned.astype(BF16), flag(down < across).astype(BF16))
    rank = jnp.where(owned > 0.0, rank, -1.0)
    mark = local.astype(F32) + 1.0
    slot = lax.broadcasted_iota(jnp.int32, (slots, edges), 0).astype(F32)
    columns = []
    for device in range(devices):
        chosen = jnp.where(rank[device : device + 1] == slot, mark[device : device + 1], 0.0)
        columns.append(jnp.sum(chosen, axis=1, keepdims=True))
    column = jnp.concatenate(columns, axis=0) - 1.0
    local_ref[...] = column
    across = lax.broadcasted_iota(jnp.int32, (devices * slots, own), 1).astype(F32)
    hot = flag(across == column).astype(BF16)
    send_ref[...] = pick(hot, parts_of(rows_ref[...], 3))


def pack_rows(first, ids, rows, slots):
    devices = ids.shape[0]
    own, width = rows.shape
    return pl.pallas_call(
        functools.partial(pack_rows_kernel, own, slots),
        out_shape=(
            jax.ShapeDtypeStruct((devices * slots, width), F32),
            jax.ShapeDtypeStruct((devices * slots, 1), F32),
        ),
        in_specs=[SMEM, VMEM, VMEM],
        out_specs=(VMEM, VMEM),
        compiler_params=pltpu.CompilerParams(vmem_limit_bytes=40 << 20),
        name="pack_rows",
    )(first, ids, rows)


def edge_kernel(
    devices, own, slots, starts, count_ref, crossed_ref, ids_ref, dest_ref, negative_ref, got_ref, near_ref, *refs
):
    joined = refs[: len(starts)]
    loss_ref, back_ref, source_ref, weight_ref, table_ref = refs[len(starts) :]
    table_ref[...] = near_ref[...]

    @pl.when(crossed_ref[0] == 1)
    def _():
        for start, piece in zip(starts, joined):
            table_ref[start : start + piece.shape[0]] = piece[...]

    edges = ids_ref.shape[1]
    height = table_ref.shape[0]
    ids = ids_ref[...]
    owner = jnp.zeros(ids.shape, F32)
    for device in range(1, devices):
        owner = owner + flag(ids >= device * own)
    down = lax.broadcasted_iota(jnp.int32, (edges, edges), 0)
    across = lax.broadcasted_iota(jnp.int32, (edges, edges), 1)
    before = flag((to_column(owner) == owner) & (down < across))
    rank = jnp.sum(before, axis=0, keepdims=True)
    place = jnp.where(rank < slots, owner * slots + rank, -1.0)
    place_column = to_column(place)
    across = lax.broadcasted_iota(jnp.int32, (edges, devices * slots), 1).astype(F32)
    source = pick(flag(across == place_column).astype(BF16), parts_of(got_ref[...], 3))
    source_ref[...] = source

    table = parts_of(table_ref[...], 3)
    scores = product(parts_of(source, 3), table, LANES)

    negative = negative_ref[...]
    low = 128
    high = height // low
    row = lax.broadcasted_iota(jnp.int32, (high, negative.shape[1]), 0)
    hot_high = flag(row == lax.shift_right_logical(negative, 7)).astype(BF16)
    row = lax.broadcasted_iota(jnp.int32, (low, negative.shape[1]), 0)
    hot_low = flag(row == (negative & (low - 1))).astype(BF16)
    grid = mxu(hot_high, hot_low, LANES)
    times = jnp.concatenate([grid[i : i + 1] for i in range(high)], axis=1)

    dest = to_column(dest_ref[...].astype(F32))
    across = lax.broadcasted_iota(jnp.int32, (edges, height), 1).astype(F32)
    hot = across == dest
    positive = jnp.sum(jnp.where(hot, scores, 0.0), axis=1, keepdims=True)
    seen = times > 0.0
    top = jnp.max(jnp.where(seen, scores, -jnp.inf), axis=1, keepdims=True)
    top = jnp.maximum(top, positive)
    power = jnp.where(seen, jnp.exp(scores - top), 0.0) * times
    power_positive = jnp.exp(positive - top)
    total = power_positive + jnp.sum(power, axis=1, keepdims=True)
    logsum = top + jnp.log(total)
    edge = lax.broadcasted_iota(jnp.int32, (edges, 1), 0)
    live = flag(edge < count_ref[0, 0])
    loss = live * (logsum - positive)
    loss_ref[...] = jnp.transpose(jnp.broadcast_to(loss, (edges, 128)))[0:1]
    scale = live / total
    dpos = live * (jnp.exp(positive - logsum) - 1.0)
    weight = power * scale + jnp.where(hot, dpos, 0.0)
    weight_ref[...] = weight

    grad = product(parts_of(weight, 2), table)
    down = lax.broadcasted_iota(jnp.int32, (devices * slots, edges), 0).astype(F32)
    back_ref[...] = pick(flag(down == place).astype(BF16), parts_of(grad, 3))


def edge_step(count, crossed, ids, dest, negative, got, table, joined, starts, devices, own):
    slots = got.shape[0] // devices
    edges = ids.shape[1]
    height, width = table.shape
    return pl.pallas_call(
        functools.partial(edge_kernel, devices, own, slots, tuple(starts)),
        out_shape=(
            jax.ShapeDtypeStruct((1, edges), F32),
            jax.ShapeDtypeStruct(got.shape, F32),
            jax.ShapeDtypeStruct((edges, width), F32),
            jax.ShapeDtypeStruct((edges, height), F32),
            jax.ShapeDtypeStruct(table.shape, F32),
        ),
        in_specs=[SMEM] * 2 + [VMEM] * (5 + len(joined)),
        out_specs=(VMEM,) * 5,
        compiler_params=pltpu.CompilerParams(vmem_limit_bytes=48 << 20),
        name="edge_step",
    )(count, crossed, ids, dest, negative, got, table, *joined)


def row_of(column):
    return jnp.transpose(jnp.broadcast_to(column, (column.shape[0], 128)))[0:1]


def column_of(row):
    return jnp.transpose(jnp.broadcast_to(row, (128, row.shape[1])))[:, 0:1]


def adagrad_rows(emb, state, grad):
    state_new = column_of(state) + jnp.mean(grad * grad, axis=1, keepdims=True)
    emb_new = emb - grad * (0.1 / (jnp.sqrt(state_new) + 1e-10))
    return emb_new, row_of(state_new)


def table_kernel(
    own, weight_ref, source_ref, table_ref, state_ref, ids_ref, new_ref, state_new_ref, used_ref
):
    ids = ids_ref[...]
    most = jnp.zeros((ids.shape[0], 1), F32)
    for device in range(ids.shape[0]):
        mine = flag((ids >= device * own) & (ids < (device + 1) * own))
        most = jnp.maximum(most, jnp.sum(mine, axis=1, keepdims=True))
    used_ref[...] = jnp.max(most, axis=0, keepdims=True)
    grad = product(parts_of(weight_ref[...], 2), parts_of(source_ref[...], 2), FIRST)
    new_ref[...], state_new_ref[...] = adagrad_rows(table_ref[...], state_ref[...], grad)


def table_step(weight, source, table, state, ids, own):
    return pl.pallas_call(
        functools.partial(table_kernel, own),
        out_shape=(
            jax.ShapeDtypeStruct(table.shape, F32),
            jax.ShapeDtypeStruct(state.shape, F32),
            jax.ShapeDtypeStruct((1, 1), F32),
        ),
        in_specs=[VMEM] * 5,
        out_specs=(VMEM,) * 3,
        compiler_params=pltpu.CompilerParams(vmem_limit_bytes=48 << 20),
        name="table_step",
    )(weight, source, table, state, ids)


def source_kernel(local_ref, back_ref, rows_ref, state_ref, new_ref, state_new_ref):
    own = rows_ref.shape[0]
    across = lax.broadcasted_iota(jnp.int32, (local_ref.shape[0], own), 1).astype(F32)
    hot = flag(across == local_ref[...]).astype(BF16)
    grad = pick(hot, parts_of(back_ref[...], 3), FIRST)
    new_ref[...], state_new_ref[...] = adagrad_rows(rows_ref[...], state_ref[...], grad)


def source_step(local, back, rows, state):
    return pl.pallas_call(
        source_kernel,
        out_shape=(
            jax.ShapeDtypeStruct(rows.shape, F32),
            jax.ShapeDtypeStruct(state.shape, F32),
        ),
        in_specs=[VMEM] * 4,
        out_specs=(VMEM, VMEM),
        compiler_params=pltpu.CompilerParams(vmem_limit_bytes=40 << 20),
        name="source_step",
    )(local, back, rows, state)


def exact(left, right, dims=ROWS):
    return lax.dot_general(left, right, dims, precision=lax.Precision.HIGHEST, preferred_element_type=F32)


def held_kernel(rows_ref, table_ref, rows_out, table_out):
    rows_out[...] = rows_ref[...]
    table_out[...] = table_ref[...]


def held(rows, table):
    return pl.pallas_call(
        held_kernel,
        out_shape=(jax.ShapeDtypeStruct(rows.shape, F32), jax.ShapeDtypeStruct(table.shape, F32)),
        in_specs=[VMEM] * 2,
        out_specs=(VMEM, VMEM),
        compiler_params=pltpu.CompilerParams(vmem_limit_bytes=40 << 20),
        name="held",
    )(rows, table)


def update_kernel(emb_ref, state_ref, grad_ref, new_ref, state_new_ref):
    new_ref[...], state_new_ref[...] = adagrad_rows(emb_ref[...], state_ref[...], grad_ref[...])


def update(emb, state, grad):
    return pl.pallas_call(
        update_kernel,
        out_shape=(jax.ShapeDtypeStruct(emb.shape, F32), jax.ShapeDtypeStruct(state.shape, F32)),
        in_specs=[VMEM] * 3,
        out_specs=(VMEM, VMEM),
        compiler_params=pltpu.CompilerParams(vmem_limit_bytes=40 << 20),
        name="update",
    )(emb, state, grad)


def everywhere(value):
    copies = jnp.broadcast_to(value, (lax.axis_size("src"),) + value.shape)
    return lax.all_to_all(copies, "src", 0, 0, tiled=True).reshape(-1, value.shape[-1])


def whole_step(rows, rows_state, table, table_state, ids, all_ids, dest, negative, count, first):
    rows, table = held(rows, table)
    piece = everywhere(rows)
    columns = jnp.arange(piece.shape[0], dtype=jnp.int32)
    sources = exact((ids[:, None] == columns[None, :]).astype(F32), piece)
    index = jnp.arange(table.shape[0], dtype=jnp.int32)
    hot_dest = (dest[:, None] == index[None, :]).astype(F32)
    hot_negative = (negative[:, None] == index[None, :]).astype(F32)
    targets = exact(hot_dest, table)
    negatives = exact(hot_negative, table)
    positive = jnp.sum(sources * targets, axis=1)
    scores = exact(sources, negatives, LANES)
    live = (jnp.arange(ids.shape[0], dtype=jnp.int32) < count).astype(F32)
    top = jnp.maximum(jnp.max(scores, axis=1), positive)
    total = jnp.exp(positive - top) + jnp.sum(jnp.exp(scores - top[:, None]), axis=1)
    logsum = top + jnp.log(total)
    loss = live * (logsum - positive)
    dpos = live * (jnp.exp(positive - logsum) - 1.0)
    dneg = live[:, None] * jnp.exp(scores - logsum[:, None])
    source_grad = dpos[:, None] * targets + exact(dneg, negatives)
    dest_grad = exact(hot_dest, dpos[:, None] * sources, FIRST)
    dest_grad = dest_grad + exact(hot_negative, exact(dneg, sources, FIRST), FIRST)
    grad_piece = everywhere(source_grad)
    own_index = first + jnp.arange(rows.shape[0], dtype=jnp.int32)
    onehot = (all_ids.reshape(-1)[:, None] == own_index[None, :]).astype(F32)
    own_grad = exact(onehot, grad_piece, FIRST)
    return update(rows, rows_state, own_grad) + update(table, table_state, dest_grad) + (loss[None],)


def after(value, *others):
    return lax.optimization_barrier((value,) + others)[0]


def permute(value, axes, pairs):
    return lax.ppermute(value, axes, pairs)


def shifted(table):
    height = table.shape[0]
    wide, deep = lax.axis_size("x"), lax.axis_size("y")
    plane = wide * deep
    count = len(LEAVE)
    size = -(-height // (8 * count)) * 8
    starts = [min(size * piece, height - size) for piece in range(count)]
    spot = lambda at: (at[0] % wide) * deep + at[1] % deep
    leave, land = [spot(at) for at in LEAVE], [spot(at) for at in LAND]
    near = permute(
        table, ("zh", "x", "y"), [(j, j + 1) for j in range(2 * plane - 1) if j != plane - 1]
    )
    pieces = [table[start : start + size] for start in starts]
    spread = [permute(pieces[k], ("x", "y"), [(leave[0], leave[k])]) for k in range(1, count)]
    at = lax.axis_index("x") * deep + lax.axis_index("y")
    going = jnp.where(at == leave[0], pieces[0], sum(spread))
    come = permute(
        going,
        ("zh", "x", "y"),
        [(z * plane + leave[k], (1 - z) * plane + land[k]) for z in range(2) for k in range(count)],
    )
    joined = [come] + [permute(come, ("x", "y"), [(land[k], land[0])]) for k in range(1, count)]
    return near, joined, starts, (at == land[0]).astype(jnp.int32), going


def on_device(src_emb, src_state, dst_emb, dst_state, src_ids, dst_ids, neg_ids, counts):
    devices = lax.axis_size("src")
    behind = lax.axis_size("zh") * lax.axis_size("x") * lax.axis_size("y")
    pairs = [(source, (source + 1) % behind) for source in range(behind)]
    rows, rows_state = src_emb[0, 0], src_state[0]
    own, width = rows.shape
    ids = src_ids[0]
    first = lax.axis_index("src") * own
    all_ids = lax.all_to_all(jnp.broadcast_to(ids, (devices, ids.shape[1])), "src", 0, 0, tiled=True)
    near, joined, starts, crossed, going = shifted(dst_emb[0, 0])

    send, local = pack_rows(first.reshape(1), all_ids, rows, SLOTS)
    table_state = permute(after(dst_state[0], local), ("zh", "x", "y"), pairs)
    got = lax.all_to_all(after(send, going), "src", 0, 0, tiled=True)
    loss, back, source, weight, table = edge_step(
        counts, crossed.reshape(1), ids, dst_ids[0], neg_ids[0], got, near, joined, starts, devices, own
    )
    back = lax.all_to_all(back, "src", 0, 0, tiled=True)
    dst_new, dst_state_new, over = table_step(weight, source, table, table_state, all_ids, own)
    src_new, src_state_new = source_step(local, back, rows, rows_state)

    def again(carry):
        found = whole_step(
            rows, rows_state, table, table_state, ids[0], all_ids, dst_ids[0, 0], neg_ids[0, 0], counts[0, 0], first
        )
        return (jnp.float32(0.0),) + found

    fast = (over[0, 0], src_new, src_state_new, dst_new, dst_state_new, loss)
    done = lax.while_loop(lambda carry: carry[0] > SLOTS, again, fast)
    src_new, src_state_new, dst_new, dst_state_new, loss = done[1:]
    return src_new[None, None], src_state_new[None], dst_new[None, None], dst_state_new[None], loss[None]


def solution(mesh):
    sources, dests = mesh.devices.shape
    side = int(math.isqrt(dests // 2))
    mesh = Mesh(mesh.devices.reshape(sources, 2, side, side), ("src", "zh", "x", "y"))
    spec = lambda rank: P("src", ("zh", "x", "y"), *([None] * (rank - 2)))
    return jax.shard_map(
        on_device,
        mesh=mesh,
        in_specs=tuple(spec(rank) for rank in (4, 3, 4, 3, 3, 3, 3, 2)),
        out_specs=tuple(spec(rank) for rank in (4, 3, 4, 3, 3)),
        check_vma=False,
    )
```

```python
import functools
import math

import jax
import jax.numpy as jnp
from jax import lax
from jax.experimental import pallas as pl
from jax.experimental.pallas import tpu as pltpu
from jax.sharding import Mesh, PartitionSpec as P

SLOTS = 56
BACK_SLOTS = 40
LEAVE = ((-1, -1), (-1, 0), (0, -1), (-1, -2), (-2, -1), (0, 0))
LAND = ((0, 0), (-1, 0), (0, -1), (0, 1), (1, 0), (1, 1))
SRC = ("zl", "core")
DST = ("zh", "x", "y")
F32 = jnp.float32
BF16 = jnp.bfloat16
VMEM = pl.BlockSpec(memory_space=pltpu.VMEM)
SMEM = pl.BlockSpec(memory_space=pltpu.SMEM)
ROWS = (((1,), (0,)), ((), ()))
LANES = (((1,), (1,)), ((), ()))
FIRST = (((0,), (0,)), ((), ()))


def mxu(left, right, dims=ROWS):
    return lax.dot_general(left, right, dims, preferred_element_type=F32)


def parts_of(value, count):
    parts = []
    for _ in range(count - 1):
        part = value.astype(BF16)
        parts.append(part)
        value = value - part.astype(F32)
    parts.append(value.astype(BF16))
    return parts


def pick(onehot, parts, dims=ROWS):
    total = mxu(onehot, parts[-1], dims)
    for part in parts[-2::-1]:
        total = total + mxu(onehot, part, dims)
    return total


def product(left, right, dims=ROWS):
    total = mxu(left[0], right[1], dims) + mxu(left[1], right[0], dims)
    if len(left) > 2:
        small = mxu(left[0], right[2], dims) + mxu(left[2], right[0], dims)
        total = (small + mxu(left[1], right[1], dims)) + total
    return total + mxu(left[0], right[0], dims)


def flag(condition):
    return jnp.where(condition, 1.0, 0.0).astype(F32)


def to_column(row):
    size = row.shape[1]
    down = lax.broadcasted_iota(jnp.int32, (size, size), 0)
    across = lax.broadcasted_iota(jnp.int32, (size, size), 1)
    return jnp.sum(jnp.where(down == across, row, 0.0), axis=1, keepdims=True)


def slot_column(rank, mark, slots):
    slot = lax.broadcasted_iota(jnp.int32, (slots, rank.shape[1]), 0).astype(F32)
    columns = []
    for device in range(rank.shape[0]):
        chosen = jnp.where(rank[device : device + 1] == slot, mark[device : device + 1], 0.0)
        columns.append(jnp.sum(chosen, axis=1, keepdims=True))
    return jnp.concatenate(columns, axis=0) - 1.0


def rank_of(owned):
    edges = owned.shape[1]
    down = lax.broadcasted_iota(jnp.int32, (edges, edges), 0)
    across = lax.broadcasted_iota(jnp.int32, (edges, edges), 1)
    rank = mxu(owned.astype(BF16), flag(down < across).astype(BF16))
    return jnp.where(owned > 0.0, rank, -1.0)


def pack_rows_kernel(slots, place_ref, ids_ref, rows_ref, other_ref, send_ref):
    own = rows_ref.shape[0]
    first, first_other = place_ref[0], place_ref[1]
    pairs = [[ids_ref[core + 2 * chip : core + 2 * chip + 1] for chip in range(ids_ref.shape[0] // 2)] for core in (0, 1)]
    ids = jnp.where(place_ref[2] == 0, jnp.concatenate(pairs[0], axis=0), jnp.concatenate(pairs[1], axis=0))
    local, beside = ids - first, ids - first_other
    mine = (local >= 0) & (local < own)
    near = (beside >= 0) & (beside < own)
    mark = jnp.where(mine, local + 1, beside + (own + 1)).astype(F32)
    column = slot_column(rank_of(flag(mine | near)), mark, slots)
    across = lax.broadcasted_iota(jnp.int32, (column.shape[0], own), 1).astype(F32)
    hot = flag(across == column).astype(BF16)
    hot_other = flag(across == column - float(own)).astype(BF16)
    rows, other = parts_of(rows_ref[...], 3), parts_of(other_ref[...], 3)
    send_ref[...] = pick(hot, rows) + pick(hot_other, other)


def pack_rows(place, ids, rows, other, slots):
    chips = ids.shape[0] // 2
    return pl.pallas_call(
        functools.partial(pack_rows_kernel, slots),
        out_shape=jax.ShapeDtypeStruct((chips * slots, rows.shape[1]), F32),
        in_specs=[SMEM, VMEM, VMEM, VMEM],
        out_specs=VMEM,
        compiler_params=pltpu.CompilerParams(vmem_limit_bytes=16 << 20),
        name="pack_rows",
    )(place, ids, rows, other)


def place_of(ids, span, owners, slots):
    edges = ids.shape[1]
    owner = jnp.zeros(ids.shape, F32)
    for device in range(1, owners):
        owner = owner + flag(ids >= device * span)
    owner = jnp.where(ids >= 0, owner, -1.0)
    down = lax.broadcasted_iota(jnp.int32, (edges, edges), 0)
    across = lax.broadcasted_iota(jnp.int32, (edges, edges), 1)
    before = flag((to_column(owner) == owner) & (down < across))
    rank = jnp.sum(before, axis=0, keepdims=True)
    return jnp.where((rank < slots) & (owner >= 0.0), owner * slots + rank, -1.0)


def edge_kernel(
    own, slots, back_slots, starts, count_ref, crossed_ref, ids_ref, dest_ref, negative_ref, got_ref, near_ref, *refs
):
    joined = refs[: len(starts)]
    loss_ref, back_ref, source_ref, weight_ref, table_ref, done = refs[len(starts) :]
    table_ref[...] = near_ref[...]

    @pl.when(crossed_ref[0] == 1)
    def _():
        for start, piece in zip(starts, joined):
            rows = table_ref.at[start : start + piece.shape[0]]
            copy = pltpu.make_async_copy(piece, rows, done)
            copy.start()
            copy.wait()

    edges = ids_ref.shape[1]
    height = table_ref.shape[0]
    ids = ids_ref[...]
    got_rows, back_rows = got_ref.shape[0], back_ref.shape[0]
    place_column = to_column(place_of(ids, 2 * own, got_rows // slots, slots))
    place = place_of(ids, own, back_rows // back_slots, back_slots)
    across = lax.broadcasted_iota(jnp.int32, (edges, got_rows), 1).astype(F32)
    source = pick(flag(across == place_column).astype(BF16), parts_of(got_ref[...], 3))
    source_ref[...] = source

    table = parts_of(table_ref[...], 3)
    scores = product(parts_of(source, 3), table, LANES)

    negative = negative_ref[...]
    low = 128
    high = height // low
    row = lax.broadcasted_iota(jnp.int32, (high, negative.shape[1]), 0)
    hot_high = flag(row == lax.shift_right_logical(negative, 7)).astype(BF16)
    row = lax.broadcasted_iota(jnp.int32, (low, negative.shape[1]), 0)
    hot_low = flag(row == (negative & (low - 1))).astype(BF16)
    grid = mxu(hot_high, hot_low, LANES)
    times = jnp.concatenate([grid[i : i + 1] for i in range(high)], axis=1)

    dest = to_column(dest_ref[...].astype(F32))
    across = lax.broadcasted_iota(jnp.int32, (edges, height), 1).astype(F32)
    hot = across == dest
    positive = jnp.sum(jnp.where(hot, scores, 0.0), axis=1, keepdims=True)
    seen = times > 0.0
    top = jnp.max(jnp.where(seen, scores, -jnp.inf), axis=1, keepdims=True)
    top = jnp.maximum(top, positive)
    power = jnp.where(seen, jnp.exp(scores - top), 0.0) * times
    power_positive = jnp.exp(positive - top)
    total = power_positive + jnp.sum(power, axis=1, keepdims=True)
    logsum = top + jnp.log(total)
    edge = lax.broadcasted_iota(jnp.int32, (edges, 1), 0)
    live = flag(edge < count_ref[0, 0])
    loss = live * (logsum - positive)
    loss_ref[...] = jnp.transpose(jnp.broadcast_to(loss, (edges, 128)))[0:1]
    scale = live / total
    dpos = live * (jnp.exp(positive - logsum) - 1.0)
    weight = power * scale + jnp.where(hot, dpos, 0.0)
    weight_ref[...] = weight

    grad = product(parts_of(weight, 2), table)
    down = lax.broadcasted_iota(jnp.int32, (back_rows, edges), 0).astype(F32)
    back_ref[...] = pick(flag(down == place).astype(BF16), parts_of(grad, 3))


def edge_step(count, crossed, ids, dest, negative, got, table, joined, starts, devices, own):
    edges = ids.shape[1]
    height, width = table.shape
    return pl.pallas_call(
        functools.partial(edge_kernel, own, SLOTS, BACK_SLOTS, tuple(starts)),
        out_shape=(
            jax.ShapeDtypeStruct((1, edges), F32),
            jax.ShapeDtypeStruct((devices * BACK_SLOTS, width), F32),
            jax.ShapeDtypeStruct((edges, width), F32),
            jax.ShapeDtypeStruct((edges, height), F32),
            jax.ShapeDtypeStruct(table.shape, F32),
        ),
        in_specs=[SMEM] * 2 + [VMEM] * 5 + [pl.BlockSpec(memory_space=pl.ANY)] * len(joined),
        out_specs=(VMEM,) * 5,
        scratch_shapes=[pltpu.SemaphoreType.DMA],
        compiler_params=pltpu.CompilerParams(vmem_limit_bytes=24 << 20),
        name="edge_step",
    )(count, crossed, ids, dest, negative, got, table, *joined)


def row_of(column):
    return jnp.transpose(jnp.broadcast_to(column, (column.shape[0], 128)))[0:1]


def column_of(row):
    return jnp.transpose(jnp.broadcast_to(row, (128, row.shape[1])))[:, 0:1]


def adagrad_rows(emb, state, grad):
    state_new = column_of(state) + jnp.mean(grad * grad, axis=1, keepdims=True)
    emb_new = emb - grad * (0.1 / (jnp.sqrt(state_new) + 1e-10))
    return emb_new, row_of(state_new)


def table_kernel(
    own, slots, back_slots, first_ref, weight_ref, source_ref, table_ref, state_ref, ids_ref,
    new_ref, state_new_ref, used_ref, local_ref,
):
    ids = ids_ref[...]
    devices = ids.shape[0]
    most = jnp.zeros((devices, 1), F32)
    for chip in range(devices // 2):
        counts = []
        for device in (2 * chip, 2 * chip + 1):
            mine = flag((ids >= device * own) & (ids < (device + 1) * own))
            counts.append(jnp.sum(mine, axis=1, keepdims=True))
            most = jnp.maximum(most, counts[-1] - back_slots)
        most = jnp.maximum(most, counts[0] + counts[1] - slots)
    used_ref[...] = jnp.max(most, axis=0, keepdims=True)
    local = ids - first_ref[0]
    rank = rank_of(flag((local >= 0) & (local < own)))
    local_ref[...] = slot_column(rank, local.astype(F32) + 1.0, back_slots)
    grad = product(parts_of(weight_ref[...], 2), parts_of(source_ref[...], 2), FIRST)
    new_ref[...], state_new_ref[...] = adagrad_rows(table_ref[...], state_ref[...], grad)


def table_step(place, weight, source, table, state, ids, own):
    return pl.pallas_call(
        functools.partial(table_kernel, own, SLOTS, BACK_SLOTS),
        out_shape=(
            jax.ShapeDtypeStruct(table.shape, F32),
            jax.ShapeDtypeStruct(state.shape, F32),
            jax.ShapeDtypeStruct((1, 1), F32),
            jax.ShapeDtypeStruct((ids.shape[0] * BACK_SLOTS, 1), F32),
        ),
        in_specs=[SMEM] + [VMEM] * 5,
        out_specs=(VMEM,) * 4,
        compiler_params=pltpu.CompilerParams(vmem_limit_bytes=24 << 20),
        name="table_step",
    )(place, weight, source, table, state, ids)


def source_kernel(local_ref, back_ref, rows_ref, state_ref, new_ref, state_new_ref):
    own = rows_ref.shape[0]
    across = lax.broadcasted_iota(jnp.int32, (local_ref.shape[0], own), 1).astype(F32)
    hot = flag(across == local_ref[...]).astype(BF16)
    grad = pick(hot, parts_of(back_ref[...], 3), FIRST)
    new_ref[...], state_new_ref[...] = adagrad_rows(rows_ref[...], state_ref[...], grad)


def source_step(local, back, rows, state):
    return pl.pallas_call(
        source_kernel,
        out_shape=(
            jax.ShapeDtypeStruct(rows.shape, F32),
            jax.ShapeDtypeStruct(state.shape, F32),
        ),
        in_specs=[VMEM] * 4,
        out_specs=(VMEM, VMEM),
        compiler_params=pltpu.CompilerParams(vmem_limit_bytes=16 << 20),
        name="source_step",
    )(local, back, rows, state)


def exact(left, right, dims=ROWS):
    return lax.dot_general(left, right, dims, precision=lax.Precision.HIGHEST, preferred_element_type=F32)


def held_kernel(rows_ref, table_ref, rows_out, table_out):
    rows_out[...] = rows_ref[...]
    table_out[...] = table_ref[...]


def held(rows, table):
    return pl.pallas_call(
        held_kernel,
        out_shape=(jax.ShapeDtypeStruct(rows.shape, F32), jax.ShapeDtypeStruct(table.shape, F32)),
        in_specs=[VMEM] * 2,
        out_specs=(VMEM, VMEM),
        compiler_params=pltpu.CompilerParams(vmem_limit_bytes=16 << 20),
        name="held",
    )(rows, table)


def update_kernel(emb_ref, state_ref, grad_ref, new_ref, state_new_ref):
    new_ref[...], state_new_ref[...] = adagrad_rows(emb_ref[...], state_ref[...], grad_ref[...])


def update(emb, state, grad):
    return pl.pallas_call(
        update_kernel,
        out_shape=(jax.ShapeDtypeStruct(emb.shape, F32), jax.ShapeDtypeStruct(state.shape, F32)),
        in_specs=[VMEM] * 3,
        out_specs=(VMEM, VMEM),
        compiler_params=pltpu.CompilerParams(vmem_limit_bytes=16 << 20),
        name="update",
    )(emb, state, grad)


def everywhere(value):
    copies = jnp.broadcast_to(value, (lax.axis_size(SRC),) + value.shape)
    return lax.all_to_all(copies, SRC, 0, 0, tiled=True).reshape(-1, value.shape[-1])


def whole_step(rows, rows_state, table, table_state, ids, all_ids, dest, negative, count, first):
    rows, table = held(rows, table)
    piece = everywhere(rows)
    columns = jnp.arange(piece.shape[0], dtype=jnp.int32)
    sources = exact((ids[:, None] == columns[None, :]).astype(F32), piece)
    index = jnp.arange(table.shape[0], dtype=jnp.int32)
    hot_dest = (dest[:, None] == index[None, :]).astype(F32)
    hot_negative = (negative[:, None] == index[None, :]).astype(F32)
    targets = exact(hot_dest, table)
    negatives = exact(hot_negative, table)
    positive = jnp.sum(sources * targets, axis=1)
    scores = exact(sources, negatives, LANES)
    live = (jnp.arange(ids.shape[0], dtype=jnp.int32) < count).astype(F32)
    top = jnp.maximum(jnp.max(scores, axis=1), positive)
    total = jnp.exp(positive - top) + jnp.sum(jnp.exp(scores - top[:, None]), axis=1)
    logsum = top + jnp.log(total)
    loss = live * (logsum - positive)
    dpos = live * (jnp.exp(positive - logsum) - 1.0)
    dneg = live[:, None] * jnp.exp(scores - logsum[:, None])
    source_grad = dpos[:, None] * targets + exact(dneg, negatives)
    dest_grad = exact(hot_dest, dpos[:, None] * sources, FIRST)
    dest_grad = dest_grad + exact(hot_negative, exact(dneg, sources, FIRST), FIRST)
    grad_piece = everywhere(source_grad)
    own_index = first + jnp.arange(rows.shape[0], dtype=jnp.int32)
    onehot = (all_ids.reshape(-1)[:, None] == own_index[None, :]).astype(F32)
    own_grad = exact(onehot, grad_piece, FIRST)
    return update(rows, rows_state, own_grad) + update(table, table_state, dest_grad) + (loss[None],)


def after(value, *others):
    return lax.optimization_barrier((value,) + others)[0]


def permute(value, axes, pairs):
    return lax.ppermute(value, axes, pairs)


def shifted(table):
    height = table.shape[0]
    wide, deep = lax.axis_size("x"), lax.axis_size("y")
    plane = wide * deep
    count = len(LEAVE)
    size = -(-height // (16 * count)) * 16
    starts = [min(size * piece, height - size) for piece in range(count)]
    spot = lambda at: (at[0] % wide) * deep + at[1] % deep
    leave, land = [spot(at) for at in LEAVE], [spot(at) for at in LAND]
    near = permute(
        table, DST, [(j, j + 1) for j in range(2 * plane - 1) if j != plane - 1]
    )
    pieces = [table[start : start + size] for start in starts]
    spread = [permute(pieces[k], ("x", "y"), [(leave[0], leave[k])]) for k in range(1, count)]
    at = lax.axis_index("x") * deep + lax.axis_index("y")
    going = jnp.where(at == leave[0], pieces[0], sum(spread))
    come = permute(
        going,
        DST,
        [(z * plane + leave[k], (1 - z) * plane + land[k]) for z in range(2) for k in range(count)],
    )
    joined = [come] + [permute(come, ("x", "y"), [(land[k], land[0])]) for k in range(1, count)]
    return near, joined, starts, (at == land[0]).astype(jnp.int32), going, come


def on_device(src_emb, src_state, dst_emb, dst_state, src_ids, dst_ids, neg_ids, counts):
    devices = lax.axis_size(SRC)
    behind = lax.axis_size(DST)
    pairs = [(source, (source + 1) % behind) for source in range(behind)]
    rows, rows_state = src_emb[0, 0], src_state[0]
    own = rows.shape[0]
    core = lax.axis_index("core")
    first = lax.axis_index(SRC) * own
    place = jnp.stack([first, first + own * (1 - 2 * core), core])
    ids = src_ids[0]
    edge = lax.broadcasted_iota(jnp.int32, ids.shape, 1)
    ids = jnp.where(edge < counts[0, 0], ids, -1)
    near, joined, starts, crossed, going, come = shifted(dst_emb[0, 0])
    other = permute(rows, "core", [(0, 1), (1, 0)])
    all_ids = jnp.broadcast_to(after(ids, going), (devices, ids.shape[1]))
    all_ids = lax.all_to_all(all_ids, SRC, 0, 0, tiled=True)

    send = pack_rows(place, all_ids, rows, other, SLOTS)
    got = lax.all_to_all(after(send, come), "zl", 0, 0, tiled=True)
    table_state = permute(after(dst_state[0], send), DST, pairs)
    loss, back, source, weight, table = edge_step(
        counts, crossed.reshape(1), ids, dst_ids[0], neg_ids[0], got, near, joined, starts, devices, own
    )
    back = lax.all_to_all(back, SRC, 0, 0, tiled=True)
    dst_new, dst_state_new, over, local = table_step(place, weight, source, table, table_state, all_ids, own)
    src_new, src_state_new = source_step(local, back, rows, rows_state)

    def again(carry):
        found = whole_step(
            rows, rows_state, table, table_state, ids[0], all_ids, dst_ids[0, 0], neg_ids[0, 0], counts[0, 0], first
        )
        return (jnp.float32(0.0),) + found

    fast = (over[0, 0], src_new, src_state_new, dst_new, dst_state_new, loss)
    done = lax.while_loop(lambda carry: carry[0] > 0.0, again, fast)
    src_new, src_state_new, dst_new, dst_state_new, loss = done[1:]
    return src_new[None, None], src_state_new[None], dst_new[None, None], dst_state_new[None], loss[None]


def solution(mesh):
    sources, dests = mesh.devices.shape
    side = math.isqrt(dests // 2)
    mesh = Mesh(mesh.devices.reshape(sources // 2, 2, 2, side, side), SRC + DST)
    spec = lambda rank: P(SRC, DST, *([None] * (rank - 2)))
    return jax.shard_map(
        on_device,
        mesh=mesh,
        in_specs=tuple(spec(rank) for rank in (4, 3, 4, 3, 3, 3, 3, 2)),
        out_specs=tuple(spec(rank) for rank in (4, 3, 4, 3, 3)),
        check_vma=False,
    )
```

```python
import functools
import math

import jax
import jax.numpy as jnp
from jax import lax
from jax.experimental import pallas as pl
from jax.experimental.pallas import tpu as pltpu
from jax.sharding import Mesh, PartitionSpec as P

SLOTS = 56
BACK_SLOTS = 40
LEAVE = ((-1, -1), (-1, 0), (0, -1), (-1, -2), (-2, -1))
LAND = ((0, 0), (-1, 0), (0, -1), (0, 1), (1, 0))
SRC = ("zl", "core")
DST = ("zh", "x", "y")
F32 = jnp.float32
BF16 = jnp.bfloat16
VMEM = pl.BlockSpec(memory_space=pltpu.VMEM)
SMEM = pl.BlockSpec(memory_space=pltpu.SMEM)
ROWS = (((1,), (0,)), ((), ()))
LANES = (((1,), (1,)), ((), ()))
FIRST = (((0,), (0,)), ((), ()))


def mxu(left, right, dims=ROWS):
    return lax.dot_general(left, right, dims, preferred_element_type=F32)


def parts_of(value, count):
    parts = []
    for _ in range(count - 1):
        part = value.astype(BF16)
        parts.append(part)
        value = value - part.astype(F32)
    parts.append(value.astype(BF16))
    return parts


def pick(onehot, parts, dims=ROWS):
    total = mxu(onehot, parts[-1], dims)
    for part in parts[-2::-1]:
        total = total + mxu(onehot, part, dims)
    return total


def product(left, right, dims=ROWS):
    total = mxu(left[0], right[1], dims) + mxu(left[1], right[0], dims)
    if len(left) > 2:
        small = mxu(left[0], right[2], dims) + mxu(left[2], right[0], dims)
        total = (small + mxu(left[1], right[1], dims)) + total
    return total + mxu(left[0], right[0], dims)


def flag(condition):
    return jnp.where(condition, 1.0, 0.0).astype(F32)


def to_column(row):
    size = row.shape[1]
    down = lax.broadcasted_iota(jnp.int32, (size, size), 0)
    across = lax.broadcasted_iota(jnp.int32, (size, size), 1)
    return jnp.sum(jnp.where(down == across, row, 0.0), axis=1, keepdims=True)


def slot_column(rank, mark, slots):
    slot = lax.broadcasted_iota(jnp.int32, (slots, rank.shape[1]), 0).astype(F32)
    columns = []
    for device in range(rank.shape[0]):
        chosen = jnp.where(rank[device : device + 1] == slot, mark[device : device + 1], 0.0)
        columns.append(jnp.sum(chosen, axis=1, keepdims=True))
    return jnp.concatenate(columns, axis=0) - 1.0


def rank_of(owned):
    edges = owned.shape[1]
    down = lax.broadcasted_iota(jnp.int32, (edges, edges), 0)
    across = lax.broadcasted_iota(jnp.int32, (edges, edges), 1)
    rank = mxu(owned.astype(BF16), flag(down < across).astype(BF16))
    return jnp.where(owned > 0.0, rank, -1.0)


def pack_rows_kernel(slots, place_ref, ids_ref, rows_ref, other_ref, send_ref):
    own = rows_ref.shape[0]
    first, first_other = place_ref[0], place_ref[1]
    pairs = [[ids_ref[core + 2 * chip : core + 2 * chip + 1] for chip in range(ids_ref.shape[0] // 2)] for core in (0, 1)]
    ids = jnp.where(place_ref[2] == 0, jnp.concatenate(pairs[0], axis=0), jnp.concatenate(pairs[1], axis=0))
    local, beside = ids - first, ids - first_other
    mine = (local >= 0) & (local < own)
    near = (beside >= 0) & (beside < own)
    mark = jnp.where(mine, local + 1, beside + (own + 1)).astype(F32)
    column = slot_column(rank_of(flag(mine | near)), mark, slots)
    across = lax.broadcasted_iota(jnp.int32, (column.shape[0], own), 1).astype(F32)
    hot = flag(across == column).astype(BF16)
    hot_other = flag(across == column - float(own)).astype(BF16)
    rows, other = parts_of(rows_ref[...], 3), parts_of(other_ref[...], 3)
    send_ref[...] = pick(hot, rows) + pick(hot_other, other)


def pack_rows(place, ids, rows, other, slots):
    chips = ids.shape[0] // 2
    return pl.pallas_call(
        functools.partial(pack_rows_kernel, slots),
        out_shape=jax.ShapeDtypeStruct((chips * slots, rows.shape[1]), F32),
        in_specs=[SMEM, VMEM, VMEM, VMEM],
        out_specs=VMEM,
        compiler_params=pltpu.CompilerParams(vmem_limit_bytes=16 << 20),
        name="pack_rows",
    )(place, ids, rows, other)


def place_of(ids, span, owners, slots):
    edges = ids.shape[1]
    owner = jnp.zeros(ids.shape, F32)
    for device in range(1, owners):
        owner = owner + flag(ids >= device * span)
    owner = jnp.where(ids >= 0, owner, -1.0)
    down = lax.broadcasted_iota(jnp.int32, (edges, edges), 0)
    across = lax.broadcasted_iota(jnp.int32, (edges, edges), 1)
    before = flag((to_column(owner) == owner) & (down < across))
    rank = jnp.sum(before, axis=0, keepdims=True)
    return jnp.where((rank < slots) & (owner >= 0.0), owner * slots + rank, -1.0)


def edge_kernel(
    own, slots, back_slots, starts, count_ref, crossed_ref, ids_ref, dest_ref, negative_ref, got_ref, near_ref, *refs
):
    joined = refs[: len(starts)]
    loss_ref, back_ref, source_ref, weight_ref, table_ref, done = refs[len(starts) :]
    table_ref[...] = near_ref[...]

    @pl.when(crossed_ref[0] == 1)
    def _():
        for start, piece in zip(starts, joined):
            rows = table_ref.at[start : start + piece.shape[0]]
            copy = pltpu.make_async_copy(piece, rows, done)
            copy.start()
            copy.wait()

    edges = ids_ref.shape[1]
    height = table_ref.shape[0]
    ids = ids_ref[...]
    got_rows, back_rows = got_ref.shape[0], back_ref.shape[0]
    place_column = to_column(place_of(ids, 2 * own, got_rows // slots, slots))
    place = place_of(ids, own, back_rows // back_slots, back_slots)
    across = lax.broadcasted_iota(jnp.int32, (edges, got_rows), 1).astype(F32)
    source = pick(flag(across == place_column).astype(BF16), parts_of(got_ref[...], 3))
    source_ref[...] = source

    table = parts_of(table_ref[...], 3)
    scores = product(parts_of(source, 3), table, LANES)

    negative = negative_ref[...]
    low = 128
    high = height // low
    row = lax.broadcasted_iota(jnp.int32, (high, negative.shape[1]), 0)
    hot_high = flag(row == lax.shift_right_logical(negative, 7)).astype(BF16)
    row = lax.broadcasted_iota(jnp.int32, (low, negative.shape[1]), 0)
    hot_low = flag(row == (negative & (low - 1))).astype(BF16)
    grid = mxu(hot_high, hot_low, LANES)
    times = jnp.concatenate([grid[i : i + 1] for i in range(high)], axis=1)

    dest = to_column(dest_ref[...].astype(F32))
    across = lax.broadcasted_iota(jnp.int32, (edges, height), 1).astype(F32)
    hot = across == dest
    positive = jnp.sum(jnp.where(hot, scores, 0.0), axis=1, keepdims=True)
    seen = times > 0.0
    top = jnp.max(jnp.where(seen, scores, -jnp.inf), axis=1, keepdims=True)
    top = jnp.maximum(top, positive)
    power = jnp.where(seen, jnp.exp(scores - top), 0.0) * times
    power_positive = jnp.exp(positive - top)
    total = power_positive + jnp.sum(power, axis=1, keepdims=True)
    logsum = top + jnp.log(total)
    edge = lax.broadcasted_iota(jnp.int32, (edges, 1), 0)
    live = flag(edge < count_ref[0, 0])
    loss = live * (logsum - positive)
    loss_ref[...] = jnp.transpose(jnp.broadcast_to(loss, (edges, 128)))[0:1]
    scale = live / total
    dpos = live * (jnp.exp(positive - logsum) - 1.0)
    weight = power * scale + jnp.where(hot, dpos, 0.0)
    weight_ref[...] = weight

    grad = product(parts_of(weight, 2), table)
    down = lax.broadcasted_iota(jnp.int32, (back_rows, edges), 0).astype(F32)
    back_ref[...] = pick(flag(down == place).astype(BF16), parts_of(grad, 3))


def edge_step(count, crossed, ids, dest, negative, got, table, joined, starts, devices, own):
    edges = ids.shape[1]
    height, width = table.shape
    return pl.pallas_call(
        functools.partial(edge_kernel, own, SLOTS, BACK_SLOTS, tuple(starts)),
        out_shape=(
            jax.ShapeDtypeStruct((1, edges), F32),
            jax.ShapeDtypeStruct((devices * BACK_SLOTS, width), F32),
            jax.ShapeDtypeStruct((edges, width), F32),
            jax.ShapeDtypeStruct((edges, height), F32),
            jax.ShapeDtypeStruct(table.shape, F32),
        ),
        in_specs=[SMEM] * 2 + [VMEM] * 5 + [pl.BlockSpec(memory_space=pl.ANY)] * len(joined),
        out_specs=(VMEM,) * 5,
        scratch_shapes=[pltpu.SemaphoreType.DMA],
        compiler_params=pltpu.CompilerParams(vmem_limit_bytes=24 << 20),
        name="edge_step",
    )(count, crossed, ids, dest, negative, got, table, *joined)


def row_of(column):
    return jnp.transpose(jnp.broadcast_to(column, (column.shape[0], 128)))[0:1]


def column_of(row):
    return jnp.transpose(jnp.broadcast_to(row, (128, row.shape[1])))[:, 0:1]


def adagrad_rows(emb, state, grad):
    state_new = column_of(state) + jnp.mean(grad * grad, axis=1, keepdims=True)
    emb_new = emb - grad * (0.1 / (jnp.sqrt(state_new) + 1e-10))
    return emb_new, row_of(state_new)


def table_kernel(
    own, slots, back_slots, first_ref, weight_ref, source_ref, table_ref, state_ref, ids_ref,
    new_ref, state_new_ref, used_ref, local_ref,
):
    ids = ids_ref[...]
    devices = ids.shape[0]
    most = jnp.zeros((devices, 1), F32)
    for chip in range(devices // 2):
        counts = []
        for device in (2 * chip, 2 * chip + 1):
            mine = flag((ids >= device * own) & (ids < (device + 1) * own))
            counts.append(jnp.sum(mine, axis=1, keepdims=True))
            most = jnp.maximum(most, counts[-1] - back_slots)
        most = jnp.maximum(most, counts[0] + counts[1] - slots)
    used_ref[...] = jnp.max(most, axis=0, keepdims=True)
    local = ids - first_ref[0]
    rank = rank_of(flag((local >= 0) & (local < own)))
    local_ref[...] = slot_column(rank, local.astype(F32) + 1.0, back_slots)
    grad = product(parts_of(weight_ref[...], 2), parts_of(source_ref[...], 2), FIRST)
    new_ref[...], state_new_ref[...] = adagrad_rows(table_ref[...], state_ref[...], grad)


def table_step(place, weight, source, table, state, ids, own):
    return pl.pallas_call(
        functools.partial(table_kernel, own, SLOTS, BACK_SLOTS),
        out_shape=(
            jax.ShapeDtypeStruct(table.shape, F32),
            jax.ShapeDtypeStruct(state.shape, F32),
            jax.ShapeDtypeStruct((1, 1), F32),
            jax.ShapeDtypeStruct((ids.shape[0] * BACK_SLOTS, 1), F32),
        ),
        in_specs=[SMEM] + [VMEM] * 5,
        out_specs=(VMEM,) * 4,
        compiler_params=pltpu.CompilerParams(vmem_limit_bytes=24 << 20),
        name="table_step",
    )(place, weight, source, table, state, ids)


def source_kernel(local_ref, back_ref, rows_ref, state_ref, new_ref, state_new_ref):
    own = rows_ref.shape[0]
    across = lax.broadcasted_iota(jnp.int32, (local_ref.shape[0], own), 1).astype(F32)
    hot = flag(across == local_ref[...]).astype(BF16)
    grad = pick(hot, parts_of(back_ref[...], 3), FIRST)
    new_ref[...], state_new_ref[...] = adagrad_rows(rows_ref[...], state_ref[...], grad)


def source_step(local, back, rows, state):
    return pl.pallas_call(
        source_kernel,
        out_shape=(
            jax.ShapeDtypeStruct(rows.shape, F32),
            jax.ShapeDtypeStruct(state.shape, F32),
        ),
        in_specs=[VMEM] * 4,
        out_specs=(VMEM, VMEM),
        compiler_params=pltpu.CompilerParams(vmem_limit_bytes=16 << 20),
        name="source_step",
    )(local, back, rows, state)


def exact(left, right, dims=ROWS):
    return lax.dot_general(left, right, dims, precision=lax.Precision.HIGHEST, preferred_element_type=F32)


def held_kernel(rows_ref, table_ref, rows_out, table_out):
    rows_out[...] = rows_ref[...]
    table_out[...] = table_ref[...]


def held(rows, table):
    return pl.pallas_call(
        held_kernel,
        out_shape=(jax.ShapeDtypeStruct(rows.shape, F32), jax.ShapeDtypeStruct(table.shape, F32)),
        in_specs=[VMEM] * 2,
        out_specs=(VMEM, VMEM),
        compiler_params=pltpu.CompilerParams(vmem_limit_bytes=16 << 20),
        name="held",
    )(rows, table)


def update_kernel(emb_ref, state_ref, grad_ref, new_ref, state_new_ref):
    new_ref[...], state_new_ref[...] = adagrad_rows(emb_ref[...], state_ref[...], grad_ref[...])


def update(emb, state, grad):
    return pl.pallas_call(
        update_kernel,
        out_shape=(jax.ShapeDtypeStruct(emb.shape, F32), jax.ShapeDtypeStruct(state.shape, F32)),
        in_specs=[VMEM] * 3,
        out_specs=(VMEM, VMEM),
        compiler_params=pltpu.CompilerParams(vmem_limit_bytes=16 << 20),
        name="update",
    )(emb, state, grad)


def everywhere(value):
    copies = jnp.broadcast_to(value, (lax.axis_size(SRC),) + value.shape)
    return lax.all_to_all(copies, SRC, 0, 0, tiled=True).reshape(-1, value.shape[-1])


def whole_step(rows, rows_state, table, table_state, ids, all_ids, dest, negative, count, first):
    rows, table = held(rows, table)
    piece = everywhere(rows)
    columns = jnp.arange(piece.shape[0], dtype=jnp.int32)
    sources = exact((ids[:, None] == columns[None, :]).astype(F32), piece)
    index = jnp.arange(table.shape[0], dtype=jnp.int32)
    hot_dest = (dest[:, None] == index[None, :]).astype(F32)
    hot_negative = (negative[:, None] == index[None, :]).astype(F32)
    targets = exact(hot_dest, table)
    negatives = exact(hot_negative, table)
    positive = jnp.sum(sources * targets, axis=1)
    scores = exact(sources, negatives, LANES)
    live = (jnp.arange(ids.shape[0], dtype=jnp.int32) < count).astype(F32)
    top = jnp.maximum(jnp.max(scores, axis=1), positive)
    total = jnp.exp(positive - top) + jnp.sum(jnp.exp(scores - top[:, None]), axis=1)
    logsum = top + jnp.log(total)
    loss = live * (logsum - positive)
    dpos = live * (jnp.exp(positive - logsum) - 1.0)
    dneg = live[:, None] * jnp.exp(scores - logsum[:, None])
    source_grad = dpos[:, None] * targets + exact(dneg, negatives)
    dest_grad = exact(hot_dest, dpos[:, None] * sources, FIRST)
    dest_grad = dest_grad + exact(hot_negative, exact(dneg, sources, FIRST), FIRST)
    grad_piece = everywhere(source_grad)
    own_index = first + jnp.arange(rows.shape[0], dtype=jnp.int32)
    onehot = (all_ids.reshape(-1)[:, None] == own_index[None, :]).astype(F32)
    own_grad = exact(onehot, grad_piece, FIRST)
    return update(rows, rows_state, own_grad) + update(table, table_state, dest_grad) + (loss[None],)


def after(value, *others):
    return lax.optimization_barrier((value,) + others)[0]


def permute(value, axes, pairs):
    return lax.ppermute(value, axes, pairs)


def shifted(table):
    height = table.shape[0]
    wide, deep = lax.axis_size("x"), lax.axis_size("y")
    plane = wide * deep
    count = len(LEAVE)
    size = -(-height // (16 * count)) * 16
    starts = [min(size * piece, height - size) for piece in range(count)]
    spot = lambda at: (at[0] % wide) * deep + at[1] % deep
    leave, land = [spot(at) for at in LEAVE], [spot(at) for at in LAND]
    near = permute(
        table, DST, [(j, j + 1) for j in range(2 * plane - 1) if j != plane - 1]
    )
    pieces = [table[start : start + size] for start in starts]
    spread = [permute(pieces[k], ("x", "y"), [(leave[0], leave[k])]) for k in range(1, count)]
    at = lax.axis_index("x") * deep + lax.axis_index("y")
    going = jnp.where(at == leave[0], pieces[0], sum(spread))
    come = permute(
        going,
        DST,
        [(z * plane + leave[k], (1 - z) * plane + land[k]) for z in range(2) for k in range(count)],
    )
    joined = [come] + [permute(come, ("x", "y"), [(land[k], land[0])]) for k in range(1, count)]
    return near, joined, starts, (at == land[0]).astype(jnp.int32), going, come


def on_device(src_emb, src_state, dst_emb, dst_state, src_ids, dst_ids, neg_ids, counts):
    devices = lax.axis_size(SRC)
    behind = lax.axis_size(DST)
    pairs = [(source, (source + 1) % behind) for source in range(behind)]
    rows, rows_state = src_emb[0, 0], src_state[0]
    own = rows.shape[0]
    core = lax.axis_index("core")
    first = lax.axis_index(SRC) * own
    place = jnp.stack([first, first + own * (1 - 2 * core), core])
    ids = src_ids[0]
    edge = lax.broadcasted_iota(jnp.int32, ids.shape, 1)
    ids = jnp.where(edge < counts[0, 0], ids, -1)
    near, joined, starts, crossed, going, come = shifted(dst_emb[0, 0])
    other = permute(rows, "core", [(0, 1), (1, 0)])
    all_ids = lax.all_to_all(jnp.broadcast_to(ids, (devices, ids.shape[1])), SRC, 0, 0, tiled=True)

    send = pack_rows(place, after(all_ids, going), rows, other, SLOTS)
    got = lax.all_to_all(after(send, come, near), "zl", 0, 0, tiled=True)
    table_state = permute(after(dst_state[0], send), DST, pairs)
    got = after(got, table_state)
    loss, back, source, weight, table = edge_step(
        counts, crossed.reshape(1), ids, dst_ids[0], neg_ids[0], got, near, joined, starts, devices, own
    )
    back = lax.all_to_all(back, SRC, 0, 0, tiled=True)
    dst_new, dst_state_new, over, local = table_step(place, weight, source, table, table_state, all_ids, own)
    src_new, src_state_new = source_step(local, back, rows, rows_state)

    def again(carry):
        found = whole_step(
            rows, rows_state, table, table_state, ids[0], all_ids, dst_ids[0, 0], neg_ids[0, 0], counts[0, 0], first
        )
        return (jnp.float32(0.0),) + found

    fast = (over[0, 0], src_new, src_state_new, dst_new, dst_state_new, loss)
    done = lax.while_loop(lambda carry: carry[0] > 0.0, again, fast)
    src_new, src_state_new, dst_new, dst_state_new, loss = done[1:]
    return src_new[None, None], src_state_new[None], dst_new[None, None], dst_state_new[None], loss[None]


def solution(mesh):
    sources, dests = mesh.devices.shape
    side = math.isqrt(dests // 2)
    mesh = Mesh(mesh.devices.reshape(sources // 2, 2, 2, side, side), SRC + DST)
    spec = lambda rank: P(SRC, DST, *([None] * (rank - 2)))
    return jax.shard_map(
        on_device,
        mesh=mesh,
        in_specs=tuple(spec(rank) for rank in (4, 3, 4, 3, 3, 3, 3, 2)),
        out_specs=tuple(spec(rank) for rank in (4, 3, 4, 3, 3)),
        check_vma=False,
    )
```

```python
import functools
import math

import jax
import jax.numpy as jnp
from jax import lax
from jax.experimental import pallas as pl
from jax.experimental.pallas import tpu as pltpu
from jax.sharding import Mesh, PartitionSpec as P

SLOTS = 56
BACK_SLOTS = 40
LEAVE = ((-1, -1), (0, -1), (-2, -1), (-1, -2), (0, -2))
SRC = ("zl", "core")
DST = ("zh", "x", "y")
F32 = jnp.float32
BF16 = jnp.bfloat16
VMEM = pl.BlockSpec(memory_space=pltpu.VMEM)
SMEM = pl.BlockSpec(memory_space=pltpu.SMEM)
ROWS = (((1,), (0,)), ((), ()))
LANES = (((1,), (1,)), ((), ()))
FIRST = (((0,), (0,)), ((), ()))


def mxu(left, right, dims=ROWS):
    return lax.dot_general(left, right, dims, preferred_element_type=F32)


def parts_of(value, count):
    parts = []
    for _ in range(count - 1):
        part = value.astype(BF16)
        parts.append(part)
        value = value - part.astype(F32)
    parts.append(value.astype(BF16))
    return parts


def pick(onehot, parts, dims=ROWS):
    total = mxu(onehot, parts[-1], dims)
    for part in parts[-2::-1]:
        total = total + mxu(onehot, part, dims)
    return total


def product(left, right, dims=ROWS):
    total = mxu(left[0], right[1], dims) + mxu(left[1], right[0], dims)
    if len(left) > 2:
        small = mxu(left[0], right[2], dims) + mxu(left[2], right[0], dims)
        total = (small + mxu(left[1], right[1], dims)) + total
    return total + mxu(left[0], right[0], dims)


def flag(condition):
    return jnp.where(condition, 1.0, 0.0).astype(F32)


def to_column(row):
    size = row.shape[1]
    down = lax.broadcasted_iota(jnp.int32, (size, size), 0)
    across = lax.broadcasted_iota(jnp.int32, (size, size), 1)
    return jnp.sum(jnp.where(down == across, row, 0.0), axis=1, keepdims=True)


def slot_column(rank, mark, slots):
    slot = lax.broadcasted_iota(jnp.int32, (slots, rank.shape[1]), 0).astype(F32)
    columns = []
    for device in range(rank.shape[0]):
        chosen = jnp.where(rank[device : device + 1] == slot, mark[device : device + 1], 0.0)
        columns.append(jnp.sum(chosen, axis=1, keepdims=True))
    return jnp.concatenate(columns, axis=0) - 1.0


def rank_of(owned):
    edges = owned.shape[1]
    down = lax.broadcasted_iota(jnp.int32, (edges, edges), 0)
    across = lax.broadcasted_iota(jnp.int32, (edges, edges), 1)
    rank = mxu(owned.astype(BF16), flag(down < across).astype(BF16))
    return jnp.where(owned > 0.0, rank, -1.0)


def pack_rows_kernel(slots, place_ref, ids_ref, rows_ref, other_ref, send_ref):
    own = rows_ref.shape[0]
    first, first_other = place_ref[0], place_ref[1]
    pairs = [[ids_ref[core + 2 * chip : core + 2 * chip + 1] for chip in range(ids_ref.shape[0] // 2)] for core in (0, 1)]
    ids = jnp.where(place_ref[2] == 0, jnp.concatenate(pairs[0], axis=0), jnp.concatenate(pairs[1], axis=0))
    local, beside = ids - first, ids - first_other
    mine = (local >= 0) & (local < own)
    near = (beside >= 0) & (beside < own)
    mark = jnp.where(mine, local + 1, beside + (own + 1)).astype(F32)
    column = slot_column(rank_of(flag(mine | near)), mark, slots)
    across = lax.broadcasted_iota(jnp.int32, (column.shape[0], own), 1).astype(F32)
    hot = flag(across == column).astype(BF16)
    hot_other = flag(across == column - float(own)).astype(BF16)
    rows, other = parts_of(rows_ref[...], 3), parts_of(other_ref[...], 3)
    send_ref[...] = pick(hot, rows) + pick(hot_other, other)


def pack_rows(place, ids, rows, other, slots):
    chips = ids.shape[0] // 2
    return pl.pallas_call(
        functools.partial(pack_rows_kernel, slots),
        out_shape=jax.ShapeDtypeStruct((chips * slots, rows.shape[1]), F32),
        in_specs=[SMEM, VMEM, VMEM, VMEM],
        out_specs=VMEM,
        compiler_params=pltpu.CompilerParams(vmem_limit_bytes=16 << 20),
        name="pack_rows",
    )(place, ids, rows, other)


def place_of(ids, span, owners, slots):
    edges = ids.shape[1]
    owner = jnp.zeros(ids.shape, F32)
    for device in range(1, owners):
        owner = owner + flag(ids >= device * span)
    owner = jnp.where(ids >= 0, owner, -1.0)
    down = lax.broadcasted_iota(jnp.int32, (edges, edges), 0)
    across = lax.broadcasted_iota(jnp.int32, (edges, edges), 1)
    before = flag((to_column(owner) == owner) & (down < across))
    rank = jnp.sum(before, axis=0, keepdims=True)
    return jnp.where((rank < slots) & (owner >= 0.0), owner * slots + rank, -1.0)


def join_kernel(starts, crossed_ref, near_ref, *refs):
    joined = refs[: len(starts)]
    table_ref, state_ref, full_ref, done = refs[len(starts) :]
    height, width = table_ref.shape
    full_ref[...] = near_ref[...]

    @pl.when(crossed_ref[0] == 1)
    def _():
        for start, piece in zip(starts, joined):
            copy = pltpu.make_async_copy(piece, full_ref.at[start : start + piece.shape[0]], done)
            copy.start()
            copy.wait()

    table_ref[...] = full_ref[:height]
    rows = [full_ref[row : row + 1] for row in range(height, height + height // width)]
    state_ref[...] = jnp.concatenate(rows, axis=1)


def join(crossed, near, joined, starts, height):
    return pl.pallas_call(
        functools.partial(join_kernel, tuple(starts)),
        out_shape=(
            jax.ShapeDtypeStruct((height, near.shape[1]), F32),
            jax.ShapeDtypeStruct((1, height), F32),
        ),
        in_specs=[SMEM, VMEM] + [pl.BlockSpec(memory_space=pl.ANY)] * len(joined),
        out_specs=(VMEM, VMEM),
        scratch_shapes=[pltpu.VMEM(near.shape, F32), pltpu.SemaphoreType.DMA],
        compiler_params=pltpu.CompilerParams(vmem_limit_bytes=8 << 20),
        name="join",
    )(crossed, near, *joined)


def edge_kernel(
    own, slots, back_slots, count_ref, ids_ref, dest_ref, negative_ref, got_ref, table_ref,
    loss_ref, back_ref, source_ref, weight_ref,
):
    edges = ids_ref.shape[1]
    height = table_ref.shape[0]
    ids = ids_ref[...]
    got_rows, back_rows = got_ref.shape[0], back_ref.shape[0]
    place_column = to_column(place_of(ids, 2 * own, got_rows // slots, slots))
    place = place_of(ids, own, back_rows // back_slots, back_slots)
    across = lax.broadcasted_iota(jnp.int32, (edges, got_rows), 1).astype(F32)
    source = pick(flag(across == place_column).astype(BF16), parts_of(got_ref[...], 3))
    source_ref[...] = source

    table = parts_of(table_ref[...], 3)
    scores = product(parts_of(source, 3), table, LANES)

    negative = negative_ref[...]
    low = 128
    high = height // low
    row = lax.broadcasted_iota(jnp.int32, (high, negative.shape[1]), 0)
    hot_high = flag(row == lax.shift_right_logical(negative, 7)).astype(BF16)
    row = lax.broadcasted_iota(jnp.int32, (low, negative.shape[1]), 0)
    hot_low = flag(row == (negative & (low - 1))).astype(BF16)
    grid = mxu(hot_high, hot_low, LANES)
    times = jnp.concatenate([grid[i : i + 1] for i in range(high)], axis=1)

    dest = to_column(dest_ref[...].astype(F32))
    across = lax.broadcasted_iota(jnp.int32, (edges, height), 1).astype(F32)
    hot = across == dest
    positive = jnp.sum(jnp.where(hot, scores, 0.0), axis=1, keepdims=True)
    seen = times > 0.0
    top = jnp.max(jnp.where(seen, scores, -jnp.inf), axis=1, keepdims=True)
    top = jnp.maximum(top, positive)
    power = jnp.where(seen, jnp.exp(scores - top), 0.0) * times
    power_positive = jnp.exp(positive - top)
    total = power_positive + jnp.sum(power, axis=1, keepdims=True)
    logsum = top + jnp.log(total)
    edge = lax.broadcasted_iota(jnp.int32, (edges, 1), 0)
    live = flag(edge < count_ref[0, 0])
    loss = live * (logsum - positive)
    loss_ref[...] = jnp.transpose(jnp.broadcast_to(loss, (edges, 128)))[0:1]
    scale = live / total
    dpos = live * (jnp.exp(positive - logsum) - 1.0)
    weight = power * scale + jnp.where(hot, dpos, 0.0)
    weight_ref[...] = weight

    grad = product(parts_of(weight, 2), table)
    down = lax.broadcasted_iota(jnp.int32, (back_rows, edges), 0).astype(F32)
    back_ref[...] = pick(flag(down == place).astype(BF16), parts_of(grad, 3))


def edge_step(count, ids, dest, negative, got, table, devices, own):
    edges = ids.shape[1]
    height, width = table.shape
    return pl.pallas_call(
        functools.partial(edge_kernel, own, SLOTS, BACK_SLOTS),
        out_shape=(
            jax.ShapeDtypeStruct((1, edges), F32),
            jax.ShapeDtypeStruct((devices * BACK_SLOTS, width), F32),
            jax.ShapeDtypeStruct((edges, width), F32),
            jax.ShapeDtypeStruct((edges, height), F32),
        ),
        in_specs=[SMEM] + [VMEM] * 5,
        out_specs=(VMEM,) * 4,
        compiler_params=pltpu.CompilerParams(vmem_limit_bytes=24 << 20),
        name="edge_step",
    )(count, ids, dest, negative, got, table)


def row_of(column):
    return jnp.transpose(jnp.broadcast_to(column, (column.shape[0], 128)))[0:1]


def column_of(row):
    return jnp.transpose(jnp.broadcast_to(row, (128, row.shape[1])))[:, 0:1]


def adagrad_rows(emb, state, grad):
    state_new = column_of(state) + jnp.mean(grad * grad, axis=1, keepdims=True)
    emb_new = emb - grad * (0.1 / (jnp.sqrt(state_new) + 1e-10))
    return emb_new, row_of(state_new)


def table_kernel(
    own, slots, back_slots, first_ref, weight_ref, source_ref, table_ref, state_ref, ids_ref,
    new_ref, state_new_ref, used_ref, local_ref,
):
    ids = ids_ref[...]
    devices = ids.shape[0]
    most = jnp.zeros((devices, 1), F32)
    for chip in range(devices // 2):
        counts = []
        for device in (2 * chip, 2 * chip + 1):
            mine = flag((ids >= device * own) & (ids < (device + 1) * own))
            counts.append(jnp.sum(mine, axis=1, keepdims=True))
            most = jnp.maximum(most, counts[-1] - back_slots)
        most = jnp.maximum(most, counts[0] + counts[1] - slots)
    used_ref[...] = jnp.max(most, axis=0, keepdims=True)
    local = ids - first_ref[0]
    rank = rank_of(flag((local >= 0) & (local < own)))
    local_ref[...] = slot_column(rank, local.astype(F32) + 1.0, back_slots)
    grad = product(parts_of(weight_ref[...], 2), parts_of(source_ref[...], 2), FIRST)
    new_ref[...], state_new_ref[...] = adagrad_rows(table_ref[...], state_ref[...], grad)


def table_step(place, weight, source, table, state, ids, own):
    return pl.pallas_call(
        functools.partial(table_kernel, own, SLOTS, BACK_SLOTS),
        out_shape=(
            jax.ShapeDtypeStruct(table.shape, F32),
            jax.ShapeDtypeStruct(state.shape, F32),
            jax.ShapeDtypeStruct((1, 1), F32),
            jax.ShapeDtypeStruct((ids.shape[0] * BACK_SLOTS, 1), F32),
        ),
        in_specs=[SMEM] + [VMEM] * 5,
        out_specs=(VMEM,) * 4,
        compiler_params=pltpu.CompilerParams(vmem_limit_bytes=24 << 20),
        name="table_step",
    )(place, weight, source, table, state, ids)


def source_kernel(local_ref, back_ref, rows_ref, state_ref, new_ref, state_new_ref):
    own = rows_ref.shape[0]
    across = lax.broadcasted_iota(jnp.int32, (local_ref.shape[0], own), 1).astype(F32)
    hot = flag(across == local_ref[...]).astype(BF16)
    grad = pick(hot, parts_of(back_ref[...], 3), FIRST)
    new_ref[...], state_new_ref[...] = adagrad_rows(rows_ref[...], state_ref[...], grad)


def source_step(local, back, rows, state):
    return pl.pallas_call(
        source_kernel,
        out_shape=(
            jax.ShapeDtypeStruct(rows.shape, F32),
            jax.ShapeDtypeStruct(state.shape, F32),
        ),
        in_specs=[VMEM] * 4,
        out_specs=(VMEM, VMEM),
        compiler_params=pltpu.CompilerParams(vmem_limit_bytes=16 << 20),
        name="source_step",
    )(local, back, rows, state)


def exact(left, right, dims=ROWS):
    return lax.dot_general(left, right, dims, precision=lax.Precision.HIGHEST, preferred_element_type=F32)


def held_kernel(rows_ref, table_ref, rows_out, table_out):
    rows_out[...] = rows_ref[...]
    table_out[...] = table_ref[...]


def held(rows, table):
    return pl.pallas_call(
        held_kernel,
        out_shape=(jax.ShapeDtypeStruct(rows.shape, F32), jax.ShapeDtypeStruct(table.shape, F32)),
        in_specs=[VMEM] * 2,
        out_specs=(VMEM, VMEM),
        compiler_params=pltpu.CompilerParams(vmem_limit_bytes=16 << 20),
        name="held",
    )(rows, table)


def update_kernel(emb_ref, state_ref, grad_ref, new_ref, state_new_ref):
    new_ref[...], state_new_ref[...] = adagrad_rows(emb_ref[...], state_ref[...], grad_ref[...])


def update(emb, state, grad):
    return pl.pallas_call(
        update_kernel,
        out_shape=(jax.ShapeDtypeStruct(emb.shape, F32), jax.ShapeDtypeStruct(state.shape, F32)),
        in_specs=[VMEM] * 3,
        out_specs=(VMEM, VMEM),
        compiler_params=pltpu.CompilerParams(vmem_limit_bytes=16 << 20),
        name="update",
    )(emb, state, grad)


def everywhere(value):
    copies = jnp.broadcast_to(value, (lax.axis_size(SRC),) + value.shape)
    return lax.all_to_all(copies, SRC, 0, 0, tiled=True).reshape(-1, value.shape[-1])


def whole_step(rows, rows_state, table, table_state, ids, all_ids, dest, negative, count, first):
    rows, table = held(rows, table)
    piece = everywhere(rows)
    columns = jnp.arange(piece.shape[0], dtype=jnp.int32)
    sources = exact((ids[:, None] == columns[None, :]).astype(F32), piece)
    index = jnp.arange(table.shape[0], dtype=jnp.int32)
    hot_dest = (dest[:, None] == index[None, :]).astype(F32)
    hot_negative = (negative[:, None] == index[None, :]).astype(F32)
    targets = exact(hot_dest, table)
    negatives = exact(hot_negative, table)
    positive = jnp.sum(sources * targets, axis=1)
    scores = exact(sources, negatives, LANES)
    live = (jnp.arange(ids.shape[0], dtype=jnp.int32) < count).astype(F32)
    top = jnp.maximum(jnp.max(scores, axis=1), positive)
    total = jnp.exp(positive - top) + jnp.sum(jnp.exp(scores - top[:, None]), axis=1)
    logsum = top + jnp.log(total)
    loss = live * (logsum - positive)
    dpos = live * (jnp.exp(positive - logsum) - 1.0)
    dneg = live[:, None] * jnp.exp(scores - logsum[:, None])
    source_grad = dpos[:, None] * targets + exact(dneg, negatives)
    dest_grad = exact(hot_dest, dpos[:, None] * sources, FIRST)
    dest_grad = dest_grad + exact(hot_negative, exact(dneg, sources, FIRST), FIRST)
    grad_piece = everywhere(source_grad)
    own_index = first + jnp.arange(rows.shape[0], dtype=jnp.int32)
    onehot = (all_ids.reshape(-1)[:, None] == own_index[None, :]).astype(F32)
    own_grad = exact(onehot, grad_piece, FIRST)
    return update(rows, rows_state, own_grad) + update(table, table_state, dest_grad) + (loss[None],)


def after(value, *others):
    return lax.optimization_barrier((value,) + others)[0]


def permute(value, axes, pairs):
    return lax.ppermute(value, axes, pairs)


def with_state_kernel(table_ref, state_ref, full_ref):
    height, width = table_ref.shape
    full_ref[:height] = table_ref[...]
    for row in range(height // width):
        full_ref[height + row : height + row + 1] = state_ref[:, row * width : (row + 1) * width]
    full_ref[height + height // width :] = jnp.zeros((full_ref.shape[0] - height - height // width, width), F32)


def with_state(table, state):
    height, width = table.shape
    return pl.pallas_call(
        with_state_kernel,
        out_shape=jax.ShapeDtypeStruct((height + -(-height // (8 * width)) * 8, width), F32),
        in_specs=[VMEM] * 2,
        out_specs=VMEM,
        compiler_params=pltpu.CompilerParams(vmem_limit_bytes=8 << 20),
        name="with_state",
    )(table, state)


def shifted(table):
    height = table.shape[0]
    wide, deep = lax.axis_size("x"), lax.axis_size("y")
    plane = wide * deep
    count = len(LEAVE)
    size = -(-height // (16 * count)) * 16
    starts = [min(size * piece, height - size) for piece in range(count)]
    leave = [(x % wide) * deep + y % deep for x, y in LEAVE]
    near = permute(table, DST, [(j, j + 1) for j in range(2 * plane - 1) if j != plane - 1])
    pieces = [table[start : start + size] for start in starts]
    for k in range(1, count):
        pieces[k] = permute(pieces[k], ("x", "y"), [(leave[0], leave[k])])
    joined = [permute(pieces[k], DST, [(z * plane + leave[k], (1 - z) * plane) for z in range(2)]) for k in range(count)]
    at = lax.axis_index("x") * deep + lax.axis_index("y")
    return near, joined, starts, (at == 0).astype(jnp.int32), pieces[1:]


def on_device(src_emb, src_state, dst_emb, dst_state, src_ids, dst_ids, neg_ids, counts):
    devices = lax.axis_size(SRC)
    rows, rows_state = src_emb[0, 0], src_state[0]
    own = rows.shape[0]
    core = lax.axis_index("core")
    first = lax.axis_index(SRC) * own
    place = jnp.stack([first, first + own * (1 - 2 * core), core])
    ids = src_ids[0]
    edge = lax.broadcasted_iota(jnp.int32, ids.shape, 1)
    ids = jnp.where(edge < counts[0, 0], ids, -1)
    near, joined, starts, crossed, spread = shifted(with_state(dst_emb[0, 0], dst_state[0]))
    other = permute(rows, "core", [(0, 1), (1, 0)])
    all_ids = lax.all_to_all(jnp.broadcast_to(ids, (devices, ids.shape[1])), SRC, 0, 0, tiled=True)

    send = pack_rows(place, all_ids, rows, other, SLOTS)
    got = lax.all_to_all(after(send, near, *spread), "zl", 0, 0, tiled=True)
    table, table_state = join(crossed.reshape(1), near, joined, starts, dst_emb.shape[2])
    loss, back, source, weight = edge_step(counts, ids, dst_ids[0], neg_ids[0], got, table, devices, own)
    back = lax.all_to_all(back, SRC, 0, 0, tiled=True)
    dst_new, dst_state_new, over, local = table_step(place, weight, source, table, table_state, all_ids, own)
    src_new, src_state_new = source_step(local, back, rows, rows_state)

    def again(carry):
        found = whole_step(
            rows, rows_state, table, table_state, ids[0], all_ids, dst_ids[0, 0], neg_ids[0, 0], counts[0, 0], first
        )
        return (jnp.float32(0.0),) + found

    fast = (over[0, 0], src_new, src_state_new, dst_new, dst_state_new, loss)
    done = lax.while_loop(lambda carry: carry[0] > 0.0, again, fast)
    src_new, src_state_new, dst_new, dst_state_new, loss = done[1:]
    return src_new[None, None], src_state_new[None], dst_new[None, None], dst_state_new[None], loss[None]


def solution(mesh):
    sources, dests = mesh.devices.shape
    side = math.isqrt(dests // 2)
    mesh = Mesh(mesh.devices.reshape(sources // 2, 2, 2, side, side), SRC + DST)
    spec = lambda rank: P(SRC, DST, *([None] * (rank - 2)))
    return jax.shard_map(
        on_device,
        mesh=mesh,
        in_specs=tuple(spec(rank) for rank in (4, 3, 4, 3, 3, 3, 3, 2)),
        out_specs=tuple(spec(rank) for rank in (4, 3, 4, 3, 3)),
        check_vma=False,
    )
```

```python
import functools
import math

import jax
import jax.numpy as jnp
from jax import lax
from jax.experimental import pallas as pl
from jax.experimental.pallas import tpu as pltpu
from jax.sharding import Mesh, PartitionSpec as P

SLOTS = 56
BACK_SLOTS = 40
LEAVE = ((-1, -1), (-1, 0), (0, -1), (-1, -2), (-2, -1), (-1, 1))
LAND = ((0, 0), (2, 0), (1, -1), (0, 1), (1, 0), (1, 1))
SRC = ("zl", "core")
DST = ("zh", "x", "y")
F32 = jnp.float32
BF16 = jnp.bfloat16
VMEM = pl.BlockSpec(memory_space=pltpu.VMEM)
SMEM = pl.BlockSpec(memory_space=pltpu.SMEM)
ROWS = (((1,), (0,)), ((), ()))
LANES = (((1,), (1,)), ((), ()))
FIRST = (((0,), (0,)), ((), ()))


def mxu(left, right, dims=ROWS):
    return lax.dot_general(left, right, dims, preferred_element_type=F32)


def parts_of(value, count):
    parts = []
    for _ in range(count - 1):
        part = value.astype(BF16)
        parts.append(part)
        value = value - part.astype(F32)
    parts.append(value.astype(BF16))
    return parts


def pick(onehot, parts, dims=ROWS):
    total = mxu(onehot, parts[-1], dims)
    for part in parts[-2::-1]:
        total = total + mxu(onehot, part, dims)
    return total


def product(left, right, dims=ROWS):
    total = mxu(left[0], right[1], dims) + mxu(left[1], right[0], dims)
    if len(left) > 2:
        small = mxu(left[0], right[2], dims) + mxu(left[2], right[0], dims)
        total = (small + mxu(left[1], right[1], dims)) + total
    return total + mxu(left[0], right[0], dims)


def flag(condition):
    return jnp.where(condition, 1.0, 0.0).astype(F32)


def to_column(row):
    size = row.shape[1]
    down = lax.broadcasted_iota(jnp.int32, (size, size), 0)
    across = lax.broadcasted_iota(jnp.int32, (size, size), 1)
    return jnp.sum(jnp.where(down == across, row, 0.0), axis=1, keepdims=True)


def slot_column(rank, mark, slots):
    slot = lax.broadcasted_iota(jnp.int32, (slots, rank.shape[1]), 0).astype(F32)
    columns = []
    for device in range(rank.shape[0]):
        chosen = jnp.where(rank[device : device + 1] == slot, mark[device : device + 1], 0.0)
        columns.append(jnp.sum(chosen, axis=1, keepdims=True))
    return jnp.concatenate(columns, axis=0) - 1.0


def rank_of(owned):
    edges = owned.shape[1]
    down = lax.broadcasted_iota(jnp.int32, (edges, edges), 0)
    across = lax.broadcasted_iota(jnp.int32, (edges, edges), 1)
    rank = mxu(owned.astype(BF16), flag(down < across).astype(BF16))
    return jnp.where(owned > 0.0, rank, -1.0)


def pack_rows_kernel(slots, place_ref, ids_ref, rows_ref, other_ref, send_ref):
    own = rows_ref.shape[0]
    first, first_other = place_ref[0], place_ref[1]
    pairs = [[ids_ref[core + 2 * chip : core + 2 * chip + 1] for chip in range(ids_ref.shape[0] // 2)] for core in (0, 1)]
    ids = jnp.where(place_ref[2] == 0, jnp.concatenate(pairs[0], axis=0), jnp.concatenate(pairs[1], axis=0))
    local, beside = ids - first, ids - first_other
    mine = (local >= 0) & (local < own)
    near = (beside >= 0) & (beside < own)
    mark = jnp.where(mine, local + 1, beside + (own + 1)).astype(F32)
    column = slot_column(rank_of(flag(mine | near)), mark, slots)
    across = lax.broadcasted_iota(jnp.int32, (column.shape[0], own), 1).astype(F32)
    hot = flag(across == column).astype(BF16)
    hot_other = flag(across == column - float(own)).astype(BF16)
    rows, other = parts_of(rows_ref[...], 3), parts_of(other_ref[...], 3)
    send_ref[...] = pick(hot, rows) + pick(hot_other, other)


def pack_rows(place, ids, rows, other, slots):
    chips = ids.shape[0] // 2
    return pl.pallas_call(
        functools.partial(pack_rows_kernel, slots),
        out_shape=jax.ShapeDtypeStruct((chips * slots, rows.shape[1]), F32),
        in_specs=[SMEM, VMEM, VMEM, VMEM],
        out_specs=VMEM,
        compiler_params=pltpu.CompilerParams(vmem_limit_bytes=8 << 20),
        name="pack_rows",
    )(place, ids, rows, other)


def place_of(ids, span, owners, slots):
    edges = ids.shape[1]
    owner = jnp.zeros(ids.shape, F32)
    for device in range(1, owners):
        owner = owner + flag(ids >= device * span)
    owner = jnp.where(ids >= 0, owner, -1.0)
    down = lax.broadcasted_iota(jnp.int32, (edges, edges), 0)
    across = lax.broadcasted_iota(jnp.int32, (edges, edges), 1)
    before = flag((to_column(owner) == owner) & (down < across))
    rank = jnp.sum(before, axis=0, keepdims=True)
    return jnp.where((rank < slots) & (owner >= 0.0), owner * slots + rank, -1.0)


def join_kernel(starts, crossed_ref, near_ref, *refs):
    joined = refs[: len(starts)]
    table_ref, state_ref, full_ref, done = refs[len(starts) :]
    height, width = table_ref.shape
    full_ref[...] = near_ref[...]

    @pl.when(crossed_ref[0] == 1)
    def _():
        for start, piece in zip(starts, joined):
            copy = pltpu.make_async_copy(piece, full_ref.at[start : start + piece.shape[0]], done)
            copy.start()
            copy.wait()

    table_ref[...] = full_ref[:height]
    rows = [full_ref[row : row + 1] for row in range(height, height + height // width)]
    state_ref[...] = jnp.concatenate(rows, axis=1)


def join(crossed, near, joined, starts, height):
    return pl.pallas_call(
        functools.partial(join_kernel, tuple(starts)),
        out_shape=(
            jax.ShapeDtypeStruct((height, near.shape[1]), F32),
            jax.ShapeDtypeStruct((1, height), F32),
        ),
        in_specs=[SMEM, VMEM] + [pl.BlockSpec(memory_space=pl.ANY)] * len(joined),
        out_specs=(VMEM, VMEM),
        scratch_shapes=[pltpu.VMEM(near.shape, F32), pltpu.SemaphoreType.DMA],
        compiler_params=pltpu.CompilerParams(vmem_limit_bytes=8 << 20),
        name="join",
    )(crossed, near, *joined)


def edge_kernel(
    own, slots, back_slots, count_ref, ids_ref, dest_ref, negative_ref, got_ref, table_ref,
    loss_ref, back_ref, source_ref, weight_ref,
):
    edges = ids_ref.shape[1]
    height = table_ref.shape[0]
    ids = ids_ref[...]
    got_rows, back_rows = got_ref.shape[0], back_ref.shape[0]
    place_column = to_column(place_of(ids, 2 * own, got_rows // slots, slots))
    place = place_of(ids, own, back_rows // back_slots, back_slots)
    across = lax.broadcasted_iota(jnp.int32, (edges, got_rows), 1).astype(F32)
    source = pick(flag(across == place_column).astype(BF16), parts_of(got_ref[...], 3))
    source_ref[...] = source

    table = parts_of(table_ref[...], 3)
    scores = product(parts_of(source, 3), table, LANES)

    negative = negative_ref[...]
    low = 128
    high = height // low
    row = lax.broadcasted_iota(jnp.int32, (high, negative.shape[1]), 0)
    hot_high = flag(row == lax.shift_right_logical(negative, 7)).astype(BF16)
    row = lax.broadcasted_iota(jnp.int32, (low, negative.shape[1]), 0)
    hot_low = flag(row == (negative & (low - 1))).astype(BF16)
    grid = mxu(hot_high, hot_low, LANES)
    times = jnp.concatenate([grid[i : i + 1] for i in range(high)], axis=1)

    dest = to_column(dest_ref[...].astype(F32))
    across = lax.broadcasted_iota(jnp.int32, (edges, height), 1).astype(F32)
    hot = across == dest
    positive = jnp.sum(jnp.where(hot, scores, 0.0), axis=1, keepdims=True)
    seen = times > 0.0
    top = jnp.max(jnp.where(seen, scores, -jnp.inf), axis=1, keepdims=True)
    top = jnp.maximum(top, positive)
    power = jnp.where(seen, jnp.exp(scores - top), 0.0) * times
    power_positive = jnp.exp(positive - top)
    total = power_positive + jnp.sum(power, axis=1, keepdims=True)
    logsum = top + jnp.log(total)
    edge = lax.broadcasted_iota(jnp.int32, (edges, 1), 0)
    live = flag(edge < count_ref[0, 0])
    loss = live * (logsum - positive)
    loss_ref[...] = jnp.transpose(jnp.broadcast_to(loss, (edges, 128)))[0:1]
    scale = live / total
    dpos = live * (jnp.exp(positive - logsum) - 1.0)
    weight = power * scale + jnp.where(hot, dpos, 0.0)
    weight_ref[...] = weight

    grad = product(parts_of(weight, 2), table)
    down = lax.broadcasted_iota(jnp.int32, (back_rows, edges), 0).astype(F32)
    back_ref[...] = pick(flag(down == place).astype(BF16), parts_of(grad, 3))


def edge_step(count, ids, dest, negative, got, table, devices, own):
    edges = ids.shape[1]
    height, width = table.shape
    return pl.pallas_call(
        functools.partial(edge_kernel, own, SLOTS, BACK_SLOTS),
        out_shape=(
            jax.ShapeDtypeStruct((1, edges), F32),
            jax.ShapeDtypeStruct((devices * BACK_SLOTS, width), F32),
            jax.ShapeDtypeStruct((edges, width), F32),
            jax.ShapeDtypeStruct((edges, height), F32),
        ),
        in_specs=[SMEM] + [VMEM] * 5,
        out_specs=(VMEM,) * 4,
        compiler_params=pltpu.CompilerParams(vmem_limit_bytes=16 << 20),
        name="edge_step",
    )(count, ids, dest, negative, got, table)


def row_of(column):
    return jnp.transpose(jnp.broadcast_to(column, (column.shape[0], 128)))[0:1]


def column_of(row):
    return jnp.transpose(jnp.broadcast_to(row, (128, row.shape[1])))[:, 0:1]


def adagrad_rows(emb, state, grad):
    state_new = column_of(state) + jnp.mean(grad * grad, axis=1, keepdims=True)
    emb_new = emb - grad * (0.1 / (jnp.sqrt(state_new) + 1e-10))
    return emb_new, row_of(state_new)


def table_kernel(
    own, slots, back_slots, first_ref, weight_ref, source_ref, table_ref, state_ref, ids_ref,
    new_ref, state_new_ref, used_ref, local_ref,
):
    ids = ids_ref[...]
    devices = ids.shape[0]
    most = jnp.zeros((devices, 1), F32)
    for chip in range(devices // 2):
        counts = []
        for device in (2 * chip, 2 * chip + 1):
            mine = flag((ids >= device * own) & (ids < (device + 1) * own))
            counts.append(jnp.sum(mine, axis=1, keepdims=True))
            most = jnp.maximum(most, counts[-1] - back_slots)
        most = jnp.maximum(most, counts[0] + counts[1] - slots)
    used_ref[...] = jnp.max(most, axis=0, keepdims=True)
    local = ids - first_ref[0]
    rank = rank_of(flag((local >= 0) & (local < own)))
    local_ref[...] = slot_column(rank, local.astype(F32) + 1.0, back_slots)
    grad = product(parts_of(weight_ref[...], 2), parts_of(source_ref[...], 2), FIRST)
    new_ref[...], state_new_ref[...] = adagrad_rows(table_ref[...], state_ref[...], grad)


def table_step(place, weight, source, table, state, ids, own):
    return pl.pallas_call(
        functools.partial(table_kernel, own, SLOTS, BACK_SLOTS),
        out_shape=(
            jax.ShapeDtypeStruct(table.shape, F32),
            jax.ShapeDtypeStruct(state.shape, F32),
            jax.ShapeDtypeStruct((1, 1), F32),
            jax.ShapeDtypeStruct((ids.shape[0] * BACK_SLOTS, 1), F32),
        ),
        in_specs=[SMEM] + [VMEM] * 5,
        out_specs=(VMEM,) * 4,
        compiler_params=pltpu.CompilerParams(vmem_limit_bytes=16 << 20),
        name="table_step",
    )(place, weight, source, table, state, ids)


def source_kernel(local_ref, back_ref, rows_ref, state_ref, new_ref, state_new_ref):
    own = rows_ref.shape[0]
    across = lax.broadcasted_iota(jnp.int32, (local_ref.shape[0], own), 1).astype(F32)
    hot = flag(across == local_ref[...]).astype(BF16)
    grad = pick(hot, parts_of(back_ref[...], 3), FIRST)
    new_ref[...], state_new_ref[...] = adagrad_rows(rows_ref[...], state_ref[...], grad)


def source_step(local, back, rows, state):
    return pl.pallas_call(
        source_kernel,
        out_shape=(
            jax.ShapeDtypeStruct(rows.shape, F32),
            jax.ShapeDtypeStruct(state.shape, F32),
        ),
        in_specs=[VMEM] * 4,
        out_specs=(VMEM, VMEM),
        compiler_params=pltpu.CompilerParams(vmem_limit_bytes=8 << 20),
        name="source_step",
    )(local, back, rows, state)


def exact(left, right, dims=ROWS):
    return lax.dot_general(left, right, dims, precision=lax.Precision.HIGHEST, preferred_element_type=F32)


def held_kernel(rows_ref, table_ref, rows_out, table_out):
    rows_out[...] = rows_ref[...]
    table_out[...] = table_ref[...]


def held(rows, table):
    return pl.pallas_call(
        held_kernel,
        out_shape=(jax.ShapeDtypeStruct(rows.shape, F32), jax.ShapeDtypeStruct(table.shape, F32)),
        in_specs=[VMEM] * 2,
        out_specs=(VMEM, VMEM),
        compiler_params=pltpu.CompilerParams(vmem_limit_bytes=8 << 20),
        name="held",
    )(rows, table)


def update_kernel(emb_ref, state_ref, grad_ref, new_ref, state_new_ref):
    new_ref[...], state_new_ref[...] = adagrad_rows(emb_ref[...], state_ref[...], grad_ref[...])


def update(emb, state, grad):
    return pl.pallas_call(
        update_kernel,
        out_shape=(jax.ShapeDtypeStruct(emb.shape, F32), jax.ShapeDtypeStruct(state.shape, F32)),
        in_specs=[VMEM] * 3,
        out_specs=(VMEM, VMEM),
        compiler_params=pltpu.CompilerParams(vmem_limit_bytes=8 << 20),
        name="update",
    )(emb, state, grad)


def everywhere(value):
    copies = jnp.broadcast_to(value, (lax.axis_size(SRC),) + value.shape)
    return lax.all_to_all(copies, SRC, 0, 0, tiled=True).reshape(-1, value.shape[-1])


def whole_step(rows, rows_state, table, table_state, ids, all_ids, dest, negative, count, first):
    rows, table = held(rows, table)
    piece = everywhere(rows)
    columns = jnp.arange(piece.shape[0], dtype=jnp.int32)
    sources = exact((ids[:, None] == columns[None, :]).astype(F32), piece)
    index = jnp.arange(table.shape[0], dtype=jnp.int32)
    hot_dest = (dest[:, None] == index[None, :]).astype(F32)
    hot_negative = (negative[:, None] == index[None, :]).astype(F32)
    targets = exact(hot_dest, table)
    negatives = exact(hot_negative, table)
    positive = jnp.sum(sources * targets, axis=1)
    scores = exact(sources, negatives, LANES)
    live = (jnp.arange(ids.shape[0], dtype=jnp.int32) < count).astype(F32)
    top = jnp.maximum(jnp.max(scores, axis=1), positive)
    total = jnp.exp(positive - top) + jnp.sum(jnp.exp(scores - top[:, None]), axis=1)
    logsum = top + jnp.log(total)
    loss = live * (logsum - positive)
    dpos = live * (jnp.exp(positive - logsum) - 1.0)
    dneg = live[:, None] * jnp.exp(scores - logsum[:, None])
    source_grad = dpos[:, None] * targets + exact(dneg, negatives)
    dest_grad = exact(hot_dest, dpos[:, None] * sources, FIRST)
    dest_grad = dest_grad + exact(hot_negative, exact(dneg, sources, FIRST), FIRST)
    grad_piece = everywhere(source_grad)
    own_index = first + jnp.arange(rows.shape[0], dtype=jnp.int32)
    onehot = (all_ids.reshape(-1)[:, None] == own_index[None, :]).astype(F32)
    own_grad = exact(onehot, grad_piece, FIRST)
    return update(rows, rows_state, own_grad) + update(table, table_state, dest_grad) + (loss[None],)


def after(value, *others):
    return lax.optimization_barrier((value,) + others)[0]


def permute(value, axes, pairs):
    return lax.ppermute(value, axes, pairs)


def with_state_kernel(table_ref, state_ref, full_ref):
    height, width = table_ref.shape
    full_ref[:height] = table_ref[...]
    for row in range(height // width):
        full_ref[height + row : height + row + 1] = state_ref[:, row * width : (row + 1) * width]
    full_ref[height + height // width :] = jnp.zeros((full_ref.shape[0] - height - height // width, width), F32)


def with_state(table, state):
    height, width = table.shape
    return pl.pallas_call(
        with_state_kernel,
        out_shape=jax.ShapeDtypeStruct((height + -(-height // (8 * width)) * 8, width), F32),
        in_specs=[VMEM] * 2,
        out_specs=VMEM,
        compiler_params=pltpu.CompilerParams(vmem_limit_bytes=8 << 20),
        name="with_state",
    )(table, state)


def shifted(table, state):
    wide, deep = lax.axis_size("x"), lax.axis_size("y")
    plane = wide * deep
    count = len(LEAVE)
    full = with_state(table, state)
    size = -(-full.shape[0] // (8 * count)) * 8
    rest = full.shape[0] - size
    starts = [rest] + [min(size * piece, rest - size) for piece in range(count - 1)]
    spot = lambda at: (at[0] % wide) * deep + at[1] % deep
    leave, land = [spot(at) for at in LEAVE], [spot(at) for at in LAND]
    spread = [
        permute(table[starts[k] : starts[k] + size], ("x", "y"), [(leave[0], leave[k])]) for k in range(1, count)
    ]
    at = lax.axis_index("x") * deep + lax.axis_index("y")
    going = jnp.where(at == leave[0], full[starts[0] :], sum(spread))
    near = permute(after(full, *spread), DST, [(j, j + 1) for j in range(2 * plane - 1) if j != plane - 1])
    come = permute(
        going,
        DST,
        [(z * plane + leave[k], (1 - z) * plane + land[k]) for z in range(2) for k in range(count)],
    )
    joined = [come] + [permute(come, ("x", "y"), [(land[k], land[0])]) for k in range(1, count)]
    return near, joined, starts, (at == land[0]).astype(jnp.int32), spread[-1]


def on_device(src_emb, src_state, dst_emb, dst_state, src_ids, dst_ids, neg_ids, counts):
    devices = lax.axis_size(SRC)
    rows, rows_state = src_emb[0, 0], src_state[0]
    own = rows.shape[0]
    core = lax.axis_index("core")
    first = lax.axis_index(SRC) * own
    place = jnp.stack([first, first + own * (1 - 2 * core), core])
    ids = src_ids[0]
    edge = lax.broadcasted_iota(jnp.int32, ids.shape, 1)
    ids = jnp.where(edge < counts[0, 0], ids, -1)
    near, joined, starts, crossed, spread = shifted(dst_emb[0, 0], dst_state[0])
    other = permute(after(rows, spread), "core", [(0, 1), (1, 0)])
    all_ids = lax.all_to_all(jnp.broadcast_to(ids, (devices, ids.shape[1])), SRC, 0, 0, tiled=True)

    send = pack_rows(place, all_ids, rows, other, SLOTS)
    got = lax.all_to_all(after(send, near, joined[0]), "zl", 0, 0, tiled=True)
    table, table_state = join(crossed.reshape(1), near, joined, starts, dst_emb.shape[2])
    loss, back, source, weight = edge_step(counts, ids, dst_ids[0], neg_ids[0], got, table, devices, own)
    back = lax.all_to_all(back, SRC, 0, 0, tiled=True)
    dst_new, dst_state_new, over, local = table_step(place, weight, source, table, table_state, all_ids, own)
    src_new, src_state_new = source_step(local, back, rows, rows_state)

    def again(carry):
        found = whole_step(
            rows, rows_state, table, table_state, ids[0], all_ids, dst_ids[0, 0], neg_ids[0, 0], counts[0, 0], first
        )
        return (jnp.float32(0.0),) + found

    fast = (over[0, 0], src_new, src_state_new, dst_new, dst_state_new, loss)
    done = lax.while_loop(lambda carry: carry[0] > 0.0, again, fast)
    src_new, src_state_new, dst_new, dst_state_new, loss = done[1:]
    return src_new[None, None], src_state_new[None], dst_new[None, None], dst_state_new[None], loss[None]


def solution(mesh):
    sources, dests = mesh.devices.shape
    side = math.isqrt(dests // 2)
    mesh = Mesh(mesh.devices.reshape(sources // 2, 2, 2, side, side), SRC + DST)
    spec = lambda rank: P(SRC, DST, *([None] * (rank - 2)))
    return jax.shard_map(
        on_device,
        mesh=mesh,
        in_specs=tuple(spec(rank) for rank in (4, 3, 4, 3, 3, 3, 3, 2)),
        out_specs=tuple(spec(rank) for rank in (4, 3, 4, 3, 3)),
        check_vma=False,
    )
```

```python
import functools
import math

import jax
import jax.numpy as jnp
from jax import lax
from jax.experimental import pallas as pl
from jax.experimental.pallas import tpu as pltpu
from jax.sharding import Mesh, PartitionSpec as P

SLOTS = 56
BACK_SLOTS = 40
LEAVE = ((-1, -1), (-1, 0), (0, -1), (-1, -2), (-2, -1), (-1, 1))
LAND = ((0, 0), (2, 0), (1, -1), (0, 1), (1, 0), (1, 1))
SRC = ("zl", "core")
DST = ("zh", "x", "y")
F32 = jnp.float32
BF16 = jnp.bfloat16
VMEM = pl.BlockSpec(memory_space=pltpu.VMEM)
SMEM = pl.BlockSpec(memory_space=pltpu.SMEM)
ROWS = (((1,), (0,)), ((), ()))
LANES = (((1,), (1,)), ((), ()))
FIRST = (((0,), (0,)), ((), ()))


def mxu(left, right, dims=ROWS):
    return lax.dot_general(left, right, dims, preferred_element_type=F32)


def parts_of(value, count):
    parts = []
    for _ in range(count - 1):
        part = value.astype(BF16)
        parts.append(part)
        value = value - part.astype(F32)
    parts.append(value.astype(BF16))
    return parts


def pick(onehot, parts, dims=ROWS):
    total = mxu(onehot, parts[-1], dims)
    for part in parts[-2::-1]:
        total = total + mxu(onehot, part, dims)
    return total


def product(left, right, dims=ROWS):
    total = mxu(left[0], right[1], dims) + mxu(left[1], right[0], dims)
    if len(left) > 2:
        small = mxu(left[0], right[2], dims) + mxu(left[2], right[0], dims)
        total = (small + mxu(left[1], right[1], dims)) + total
    return total + mxu(left[0], right[0], dims)


def flag(condition):
    return jnp.where(condition, 1.0, 0.0).astype(F32)


def to_column(row):
    size = row.shape[1]
    down = lax.broadcasted_iota(jnp.int32, (size, size), 0)
    across = lax.broadcasted_iota(jnp.int32, (size, size), 1)
    return jnp.sum(jnp.where(down == across, row, 0.0), axis=1, keepdims=True)


def slot_column(rank, mark, slots):
    slot = lax.broadcasted_iota(jnp.int32, (slots, rank.shape[1]), 0).astype(F32)
    columns = []
    for device in range(rank.shape[0]):
        chosen = jnp.where(rank[device : device + 1] == slot, mark[device : device + 1], 0.0)
        columns.append(jnp.sum(chosen, axis=1, keepdims=True))
    return jnp.concatenate(columns, axis=0) - 1.0


def rank_of(owned):
    edges = owned.shape[1]
    down = lax.broadcasted_iota(jnp.int32, (edges, edges), 0)
    across = lax.broadcasted_iota(jnp.int32, (edges, edges), 1)
    rank = mxu(owned.astype(BF16), flag(down < across).astype(BF16))
    return jnp.where(owned > 0.0, rank, -1.0)


def pack_rows_kernel(slots, place_ref, ids_ref, rows_ref, other_ref, send_ref):
    own = rows_ref.shape[0]
    first, first_other = place_ref[0], place_ref[1]
    pairs = [[ids_ref[core + 2 * chip : core + 2 * chip + 1] for chip in range(ids_ref.shape[0] // 2)] for core in (0, 1)]
    ids = jnp.where(place_ref[2] == 0, jnp.concatenate(pairs[0], axis=0), jnp.concatenate(pairs[1], axis=0))
    local, beside = ids - first, ids - first_other
    mine = (local >= 0) & (local < own)
    near = (beside >= 0) & (beside < own)
    mark = jnp.where(mine, local + 1, beside + (own + 1)).astype(F32)
    column = slot_column(rank_of(flag(mine | near)), mark, slots)
    across = lax.broadcasted_iota(jnp.int32, (column.shape[0], own), 1).astype(F32)
    hot = flag(across == column).astype(BF16)
    hot_other = flag(across == column - float(own)).astype(BF16)
    rows, other = parts_of(rows_ref[...], 3), parts_of(other_ref[...], 3)
    send_ref[...] = pick(hot, rows) + pick(hot_other, other)


def pack_rows(place, ids, rows, other, slots):
    chips = ids.shape[0] // 2
    return pl.pallas_call(
        functools.partial(pack_rows_kernel, slots),
        out_shape=jax.ShapeDtypeStruct((chips * slots, rows.shape[1]), F32),
        in_specs=[SMEM, VMEM, VMEM, VMEM],
        out_specs=VMEM,
        compiler_params=pltpu.CompilerParams(vmem_limit_bytes=4 << 20),
        name="pack_rows",
    )(place, ids, rows, other)


def place_of(ids, span, owners, slots):
    edges = ids.shape[1]
    owner = jnp.zeros(ids.shape, F32)
    for device in range(1, owners):
        owner = owner + flag(ids >= device * span)
    owner = jnp.where(ids >= 0, owner, -1.0)
    down = lax.broadcasted_iota(jnp.int32, (edges, edges), 0)
    across = lax.broadcasted_iota(jnp.int32, (edges, edges), 1)
    before = flag((to_column(owner) == owner) & (down < across))
    rank = jnp.sum(before, axis=0, keepdims=True)
    return jnp.where((rank < slots) & (owner >= 0.0), owner * slots + rank, -1.0)


def join_kernel(own, devices, slots, back_slots, starts, crossed_ref, near_ref, ids_ref, dest_ref, negative_ref, *refs):
    joined = refs[: len(starts)]
    table_ref, state_ref, parts_ref, times_ref, place_ref, full_ref, done = refs[len(starts) :]
    ids = ids_ref[...]
    place_ref[0:1] = place_of(ids, 2 * own, devices // 2, slots)
    place_ref[1:2] = place_of(ids, own, devices, back_slots)
    place_ref[2:3] = dest_ref[...].astype(F32)
    place_ref[3:] = jnp.zeros((place_ref.shape[0] - 3, ids.shape[1]), F32)

    negative = negative_ref[...]
    low = 128
    high = table_ref.shape[0] // low
    row = lax.broadcasted_iota(jnp.int32, (high, negative.shape[1]), 0)
    hot_high = flag(row == lax.shift_right_logical(negative, 7)).astype(BF16)
    row = lax.broadcasted_iota(jnp.int32, (low, negative.shape[1]), 0)
    hot_low = flag(row == (negative & (low - 1))).astype(BF16)
    grid = mxu(hot_high, hot_low, LANES)
    times_ref[...] = jnp.concatenate([grid[i : i + 1] for i in range(high)], axis=1)

    height, width = table_ref.shape
    full_ref[...] = near_ref[...]

    @pl.when(crossed_ref[0] == 1)
    def _():
        for start, piece in zip(starts, joined):
            copy = pltpu.make_async_copy(piece, full_ref.at[start : start + piece.shape[0]], done)
            copy.start()
            copy.wait()

    table = full_ref[:height]
    table_ref[...] = table
    for place, part in enumerate(parts_of(table, 3)):
        parts_ref[place] = part
    rows = [full_ref[row : row + 1] for row in range(height, height + height // width)]
    state_ref[...] = jnp.concatenate(rows, axis=1)


def join(crossed, near, ids, dest, negative, joined, starts, height, devices, own):
    edges = ids.shape[1]
    return pl.pallas_call(
        functools.partial(join_kernel, own, devices, SLOTS, BACK_SLOTS, tuple(starts)),
        out_shape=(
            jax.ShapeDtypeStruct((height, near.shape[1]), F32),
            jax.ShapeDtypeStruct((1, height), F32),
            jax.ShapeDtypeStruct((3, height, near.shape[1]), BF16),
            jax.ShapeDtypeStruct((1, height), F32),
            jax.ShapeDtypeStruct((8, edges), F32),
        ),
        in_specs=[SMEM] + [VMEM] * 4 + [pl.BlockSpec(memory_space=pl.ANY)] * len(joined),
        out_specs=(VMEM,) * 5,
        scratch_shapes=[pltpu.VMEM(near.shape, F32), pltpu.SemaphoreType.DMA],
        compiler_params=pltpu.CompilerParams(vmem_limit_bytes=8 << 20),
        name="join",
    )(crossed, near, ids, dest, negative, *joined)


def edge_kernel(
    count_ref, got_ref, parts_ref, times_ref, place_ref, loss_ref, back_ref, source_ref, weight_ref
):
    across = lax.broadcasted_iota(jnp.int32, (source_ref.shape[0], got_ref.shape[0]), 1).astype(F32)
    got_hot = flag(across == to_column(place_ref[0:1])).astype(BF16)
    source = pick(got_hot, parts_of(got_ref[...], 3))
    source_ref[...] = source
    table = [parts_ref[part] for part in range(3)]
    scores = product(parts_of(source, 3), table, LANES)
    edges, height = scores.shape
    times = times_ref[...]
    across = lax.broadcasted_iota(jnp.int32, (edges, height), 1).astype(F32)
    hot = across == to_column(place_ref[2:3])
    positive = jnp.sum(jnp.where(hot, scores, 0.0), axis=1, keepdims=True)
    seen = times > 0.0
    top = jnp.max(jnp.where(seen, scores, -jnp.inf), axis=1, keepdims=True)
    top = jnp.maximum(top, positive)
    power = jnp.where(seen, jnp.exp(scores - top), 0.0) * times
    power_positive = jnp.exp(positive - top)
    total = power_positive + jnp.sum(power, axis=1, keepdims=True)
    logsum = top + jnp.log(total)
    edge = lax.broadcasted_iota(jnp.int32, (edges, 1), 0)
    live = flag(edge < count_ref[0, 0])
    loss = live * (logsum - positive)
    loss_ref[...] = jnp.transpose(jnp.broadcast_to(loss, (edges, 128)))[0:1]
    scale = live / total
    dpos = live * (jnp.exp(positive - logsum) - 1.0)
    weight = power * scale + jnp.where(hot, dpos, 0.0)
    weight_ref[...] = weight

    grad = product(parts_of(weight, 2), table)
    down = lax.broadcasted_iota(jnp.int32, (back_ref.shape[0], edges), 0).astype(F32)
    back_hot = flag(down == place_ref[1:2]).astype(BF16)
    back_ref[...] = pick(back_hot, parts_of(grad, 2))


def edge_step(count, got, parts, times, place, devices):
    edges = place.shape[1]
    height, width = parts.shape[1:]
    return pl.pallas_call(
        edge_kernel,
        out_shape=(
            jax.ShapeDtypeStruct((1, edges), F32),
            jax.ShapeDtypeStruct((devices * BACK_SLOTS, width), F32),
            jax.ShapeDtypeStruct((edges, width), F32),
            jax.ShapeDtypeStruct((edges, height), F32),
        ),
        in_specs=[SMEM] + [VMEM] * 4,
        out_specs=(VMEM,) * 4,
        compiler_params=pltpu.CompilerParams(vmem_limit_bytes=8 << 20),
        name="edge_step",
    )(count, got, parts, times, place)


def row_of(column):
    return jnp.transpose(jnp.broadcast_to(column, (column.shape[0], 128)))[0:1]


def column_of(row):
    return jnp.transpose(jnp.broadcast_to(row, (128, row.shape[1])))[:, 0:1]


def adagrad_rows(emb, state, grad):
    state_new = column_of(state) + jnp.mean(grad * grad, axis=1, keepdims=True)
    emb_new = emb - grad * (0.1 / (jnp.sqrt(state_new) + 1e-10))
    return emb_new, row_of(state_new)


def table_kernel(
    own, slots, back_slots, first_ref, weight_ref, source_ref, table_ref, state_ref, ids_ref,
    new_ref, state_new_ref, used_ref, local_ref,
):
    ids = ids_ref[...]
    devices = ids.shape[0]
    most = jnp.zeros((devices, 1), F32)
    for chip in range(devices // 2):
        counts = []
        for device in (2 * chip, 2 * chip + 1):
            mine = flag((ids >= device * own) & (ids < (device + 1) * own))
            counts.append(jnp.sum(mine, axis=1, keepdims=True))
            most = jnp.maximum(most, counts[-1] - back_slots)
        most = jnp.maximum(most, counts[0] + counts[1] - slots)
    used_ref[...] = jnp.max(most, axis=0, keepdims=True)
    local = ids - first_ref[0]
    rank = rank_of(flag((local >= 0) & (local < own)))
    row = row_of(slot_column(rank, local.astype(F32) + 1.0, back_slots))
    down = lax.broadcasted_iota(jnp.int32, local_ref.shape, 0).astype(F32)
    local_ref[...] = flag(down == row).astype(BF16)
    grad = product(parts_of(weight_ref[...], 2), parts_of(source_ref[...], 2), FIRST)
    new_ref[...], state_new_ref[...] = adagrad_rows(table_ref[...], state_ref[...], grad)


def table_step(place, weight, source, table, state, ids, own):
    return pl.pallas_call(
        functools.partial(table_kernel, own, SLOTS, BACK_SLOTS),
        out_shape=(
            jax.ShapeDtypeStruct(table.shape, F32),
            jax.ShapeDtypeStruct(state.shape, F32),
            jax.ShapeDtypeStruct((1, 1), F32),
            jax.ShapeDtypeStruct((own, ids.shape[0] * BACK_SLOTS), BF16),
        ),
        in_specs=[SMEM] + [VMEM] * 5,
        out_specs=(VMEM,) * 4,
        compiler_params=pltpu.CompilerParams(vmem_limit_bytes=8 << 20),
        name="table_step",
    )(place, weight, source, table, state, ids)


def source_kernel(local_ref, back_ref, rows_ref, state_ref, new_ref, state_new_ref):
    grad = pick(local_ref[...], parts_of(back_ref[...], 2))
    new_ref[...], state_new_ref[...] = adagrad_rows(rows_ref[...], state_ref[...], grad)


def source_step(local, back, rows, state):
    return pl.pallas_call(
        source_kernel,
        out_shape=(
            jax.ShapeDtypeStruct(rows.shape, F32),
            jax.ShapeDtypeStruct(state.shape, F32),
        ),
        in_specs=[VMEM] * 4,
        out_specs=(VMEM, VMEM),
        compiler_params=pltpu.CompilerParams(vmem_limit_bytes=4 << 20),
        name="source_step",
    )(local, back, rows, state)


def exact(left, right, dims=ROWS):
    return lax.dot_general(left, right, dims, precision=lax.Precision.HIGHEST, preferred_element_type=F32)


def held_kernel(rows_ref, table_ref, rows_out, table_out):
    rows_out[...] = rows_ref[...]
    table_out[...] = table_ref[...]


def held(rows, table):
    return pl.pallas_call(
        held_kernel,
        out_shape=(jax.ShapeDtypeStruct(rows.shape, F32), jax.ShapeDtypeStruct(table.shape, F32)),
        in_specs=[VMEM] * 2,
        out_specs=(VMEM, VMEM),
        compiler_params=pltpu.CompilerParams(vmem_limit_bytes=4 << 20),
        name="held",
    )(rows, table)


def update_kernel(emb_ref, state_ref, grad_ref, new_ref, state_new_ref):
    new_ref[...], state_new_ref[...] = adagrad_rows(emb_ref[...], state_ref[...], grad_ref[...])


def update(emb, state, grad):
    return pl.pallas_call(
        update_kernel,
        out_shape=(jax.ShapeDtypeStruct(emb.shape, F32), jax.ShapeDtypeStruct(state.shape, F32)),
        in_specs=[VMEM] * 3,
        out_specs=(VMEM, VMEM),
        compiler_params=pltpu.CompilerParams(vmem_limit_bytes=6 << 20),
        name="update",
    )(emb, state, grad)


def everywhere(value):
    copies = jnp.broadcast_to(value, (lax.axis_size(SRC),) + value.shape)
    return lax.all_to_all(copies, SRC, 0, 0, tiled=True).reshape(-1, value.shape[-1])


def whole_step(rows, rows_state, table, table_state, ids, all_ids, dest, negative, count, first):
    rows, table = held(rows, table)
    piece = everywhere(rows)
    columns = jnp.arange(piece.shape[0], dtype=jnp.int32)
    sources = exact((ids[:, None] == columns[None, :]).astype(F32), piece)
    index = jnp.arange(table.shape[0], dtype=jnp.int32)
    hot_dest = (dest[:, None] == index[None, :]).astype(F32)
    hot_negative = (negative[:, None] == index[None, :]).astype(F32)
    targets = exact(hot_dest, table)
    negatives = exact(hot_negative, table)
    positive = jnp.sum(sources * targets, axis=1)
    scores = exact(sources, negatives, LANES)
    live = (jnp.arange(ids.shape[0], dtype=jnp.int32) < count).astype(F32)
    top = jnp.maximum(jnp.max(scores, axis=1), positive)
    total = jnp.exp(positive - top) + jnp.sum(jnp.exp(scores - top[:, None]), axis=1)
    logsum = top + jnp.log(total)
    loss = live * (logsum - positive)
    dpos = live * (jnp.exp(positive - logsum) - 1.0)
    dneg = live[:, None] * jnp.exp(scores - logsum[:, None])
    source_grad = dpos[:, None] * targets + exact(dneg, negatives)
    dest_grad = exact(hot_dest, dpos[:, None] * sources, FIRST)
    dest_grad = dest_grad + exact(hot_negative, exact(dneg, sources, FIRST), FIRST)
    grad_piece = everywhere(source_grad)
    own_index = first + jnp.arange(rows.shape[0], dtype=jnp.int32)
    onehot = (all_ids.reshape(-1)[:, None] == own_index[None, :]).astype(F32)
    own_grad = exact(onehot, grad_piece, FIRST)
    return update(rows, rows_state, own_grad) + update(table, table_state, dest_grad) + (loss[None],)


def after(value, *others):
    return lax.optimization_barrier((value,) + others)[0]


def permute(value, axes, pairs):
    return lax.ppermute(value, axes, pairs)


def with_state_kernel(table_ref, state_ref, full_ref):
    height, width = table_ref.shape
    full_ref[:height] = table_ref[...]
    for row in range(height // width):
        full_ref[height + row : height + row + 1] = state_ref[:, row * width : (row + 1) * width]
    full_ref[height + height // width :] = jnp.zeros((full_ref.shape[0] - height - height // width, width), F32)


def with_state(table, state):
    height, width = table.shape
    return pl.pallas_call(
        with_state_kernel,
        out_shape=jax.ShapeDtypeStruct((height + -(-height // (8 * width)) * 8, width), F32),
        in_specs=[VMEM] * 2,
        out_specs=VMEM,
        compiler_params=pltpu.CompilerParams(vmem_limit_bytes=4 << 20),
        name="with_state",
    )(table, state)


def shifted(table, state):
    wide, deep = lax.axis_size("x"), lax.axis_size("y")
    plane = wide * deep
    count = len(LEAVE)
    full = with_state(table, state)
    size = -(-full.shape[0] // (8 * count)) * 8
    rest = full.shape[0] - size
    starts = [rest] + [min(size * piece, rest - size) for piece in range(count - 1)]
    spot = lambda at: (at[0] % wide) * deep + at[1] % deep
    leave, land = [spot(at) for at in LEAVE], [spot(at) for at in LAND]
    spread = [
        permute(table[starts[k] : starts[k] + size], ("x", "y"), [(leave[0], leave[k])]) for k in range(1, count)
    ]
    at = lax.axis_index("x") * deep + lax.axis_index("y")
    going = jnp.where(at == leave[0], full[starts[0] :], sum(spread))
    near = permute(after(full, *spread), DST, [(j, j + 1) for j in range(2 * plane - 1) if j != plane - 1])
    come = permute(
        going,
        DST,
        [(z * plane + leave[k], (1 - z) * plane + land[k]) for z in range(2) for k in range(count)],
    )
    joined = [come] + [permute(come, ("x", "y"), [(land[k], land[0])]) for k in range(1, count)]
    return near, joined, starts, (at == land[0]).astype(jnp.int32), spread[0]


def on_device(src_emb, src_state, dst_emb, dst_state, src_ids, dst_ids, neg_ids, counts):
    devices = lax.axis_size(SRC)
    rows, rows_state = src_emb[0, 0], src_state[0]
    own = rows.shape[0]
    core = lax.axis_index("core")
    first = lax.axis_index(SRC) * own
    place = jnp.stack([first, first + own * (1 - 2 * core), core])
    ids = src_ids[0]
    edge = lax.broadcasted_iota(jnp.int32, ids.shape, 1)
    ids = jnp.where(edge < counts[0, 0], ids, -1)
    near, joined, starts, crossed, spread = shifted(dst_emb[0, 0], dst_state[0])
    other = permute(after(rows, spread), "core", [(0, 1), (1, 0)])
    all_ids = lax.all_to_all(jnp.broadcast_to(ids, (devices, ids.shape[1])), SRC, 0, 0, tiled=True)

    send = pack_rows(place, all_ids, rows, other, SLOTS)
    got = lax.all_to_all(after(send, near, joined[0]), "zl", 0, 0, tiled=True)
    table, table_state, *prepared = join(
        crossed.reshape(1), near, ids, dst_ids[0], neg_ids[0], joined, starts, dst_emb.shape[2], devices, own
    )
    loss, back, source, weight = edge_step(counts, got, *prepared, devices)
    back = lax.all_to_all(back, SRC, 0, 0, tiled=True)
    dst_new, dst_state_new, over, local = table_step(place, weight, source, table, table_state, all_ids, own)
    src_new, src_state_new = source_step(local, back, rows, rows_state)

    def again(carry):
        found = whole_step(
            rows, rows_state, table, table_state, ids[0], all_ids, dst_ids[0, 0], neg_ids[0, 0], counts[0, 0], first
        )
        return (jnp.float32(0.0),) + found

    fast = (over[0, 0], src_new, src_state_new, dst_new, dst_state_new, loss)
    done = lax.while_loop(lambda carry: carry[0] > 0.0, again, fast)
    src_new, src_state_new, dst_new, dst_state_new, loss = done[1:]
    return src_new[None, None], src_state_new[None], dst_new[None, None], dst_state_new[None], loss[None]


def solution(mesh):
    sources, dests = mesh.devices.shape
    side = math.isqrt(dests // 2)
    mesh = Mesh(mesh.devices.reshape(sources // 2, 2, 2, side, side), SRC + DST)
    spec = lambda rank: P(SRC, DST, *([None] * (rank - 2)))
    return jax.shard_map(
        on_device,
        mesh=mesh,
        in_specs=tuple(spec(rank) for rank in (4, 3, 4, 3, 3, 3, 3, 2)),
        out_specs=tuple(spec(rank) for rank in (4, 3, 4, 3, 3)),
        check_vma=False,
    )
```

```python
import functools
import math

import jax
import jax.numpy as jnp
from jax import lax
from jax.experimental import pallas as pl
from jax.experimental.pallas import tpu as pltpu
from jax.sharding import Mesh, PartitionSpec as P

SLOTS = 56
BACK_SLOTS = 40
LEAVE = ((-1, -1), (-1, 0), (0, -1), (-1, -2), (-2, -1), (-1, 1))
LAND = ((0, 0), (2, 0), (1, -1), (0, 1), (1, 0), (1, 1))
SRC = ("zl", "core")
DST = ("zh", "x", "y")
F32 = jnp.float32
BF16 = jnp.bfloat16
VMEM = pl.BlockSpec(memory_space=pltpu.VMEM)
SMEM = pl.BlockSpec(memory_space=pltpu.SMEM)
ROWS = (((1,), (0,)), ((), ()))
LANES = (((1,), (1,)), ((), ()))
FIRST = (((0,), (0,)), ((), ()))


def mxu(left, right, dims=ROWS):
    return lax.dot_general(left, right, dims, preferred_element_type=F32)


def parts_of(value, count):
    parts = []
    for _ in range(count - 1):
        part = value.astype(BF16)
        parts.append(part)
        value = value - part.astype(F32)
    parts.append(value.astype(BF16))
    return parts


def pick(onehot, parts, dims=ROWS):
    total = mxu(onehot, parts[-1], dims)
    for part in parts[-2::-1]:
        total = total + mxu(onehot, part, dims)
    return total


def product(left, right, dims=ROWS):
    total = mxu(left[0], right[1], dims) + mxu(left[1], right[0], dims)
    if len(left) > 2:
        small = mxu(left[0], right[2], dims) + mxu(left[2], right[0], dims)
        total = (small + mxu(left[1], right[1], dims)) + total
    return total + mxu(left[0], right[0], dims)


def flag(condition):
    return jnp.where(condition, 1.0, 0.0).astype(F32)


def to_column(row):
    size = row.shape[1]
    down = lax.broadcasted_iota(jnp.int32, (size, size), 0)
    across = lax.broadcasted_iota(jnp.int32, (size, size), 1)
    return jnp.sum(jnp.where(down == across, row, 0.0), axis=1, keepdims=True)


def slot_column(rank, mark, slots):
    slot = lax.broadcasted_iota(jnp.int32, (slots, rank.shape[1]), 0).astype(F32)
    columns = []
    for device in range(rank.shape[0]):
        chosen = jnp.where(rank[device : device + 1] == slot, mark[device : device + 1], 0.0)
        columns.append(jnp.sum(chosen, axis=1, keepdims=True))
    return jnp.concatenate(columns, axis=0) - 1.0


def rank_of(owned):
    edges = owned.shape[1]
    down = lax.broadcasted_iota(jnp.int32, (edges, edges), 0)
    across = lax.broadcasted_iota(jnp.int32, (edges, edges), 1)
    rank = mxu(owned.astype(BF16), flag(down < across).astype(BF16))
    return jnp.where(owned > 0.0, rank, -1.0)


def pack_rows_kernel(slots, place_ref, ids_ref, rows_ref, other_ref, send_ref):
    own = rows_ref.shape[0]
    first, first_other = place_ref[0], place_ref[1]
    pairs = [[ids_ref[core + 2 * chip : core + 2 * chip + 1] for chip in range(ids_ref.shape[0] // 2)] for core in (0, 1)]
    ids = jnp.where(place_ref[2] == 0, jnp.concatenate(pairs[0], axis=0), jnp.concatenate(pairs[1], axis=0))
    local, beside = ids - first, ids - first_other
    mine = (local >= 0) & (local < own)
    near = (beside >= 0) & (beside < own)
    mark = jnp.where(mine, local + 1, beside + (own + 1)).astype(F32)
    column = slot_column(rank_of(flag(mine | near)), mark, slots)
    across = lax.broadcasted_iota(jnp.int32, (column.shape[0], own), 1).astype(F32)
    hot = flag(across == column).astype(BF16)
    hot_other = flag(across == column - float(own)).astype(BF16)
    rows, other = parts_of(rows_ref[...], 3), parts_of(other_ref[...], 3)
    send_ref[...] = pick(hot, rows) + pick(hot_other, other)


def pack_rows(place, ids, rows, other, slots):
    chips = ids.shape[0] // 2
    return pl.pallas_call(
        functools.partial(pack_rows_kernel, slots),
        out_shape=jax.ShapeDtypeStruct((chips * slots, rows.shape[1]), F32),
        in_specs=[SMEM, VMEM, VMEM, VMEM],
        out_specs=VMEM,
        compiler_params=pltpu.CompilerParams(vmem_limit_bytes=4 << 20),
        name="pack_rows",
    )(place, ids, rows, other)


def place_of(ids, span, owners, slots):
    edges = ids.shape[1]
    owner = jnp.zeros(ids.shape, F32)
    for device in range(1, owners):
        owner = owner + flag(ids >= device * span)
    owner = jnp.where(ids >= 0, owner, -1.0)
    down = lax.broadcasted_iota(jnp.int32, (edges, edges), 0)
    across = lax.broadcasted_iota(jnp.int32, (edges, edges), 1)
    before = flag((to_column(owner) == owner) & (down < across))
    rank = jnp.sum(before, axis=0, keepdims=True)
    return jnp.where((rank < slots) & (owner >= 0.0), owner * slots + rank, -1.0)


def join_kernel(own, devices, slots, back_slots, starts, crossed_ref, near_ref, ids_ref, dest_ref, negative_ref, *refs):
    joined = refs[: len(starts)]
    table_ref, state_ref, parts_ref, times_ref, place_ref, full_ref, done = refs[len(starts) :]
    ids = ids_ref[...]
    place_ref[0:1] = place_of(ids, 2 * own, devices // 2, slots)
    place_ref[1:2] = place_of(ids, own, devices, back_slots)
    place_ref[2:3] = dest_ref[...].astype(F32)
    place_ref[3:] = jnp.zeros((place_ref.shape[0] - 3, ids.shape[1]), F32)

    negative = negative_ref[...]
    low = 128
    high = table_ref.shape[0] // low
    row = lax.broadcasted_iota(jnp.int32, (high, negative.shape[1]), 0)
    hot_high = flag(row == lax.shift_right_logical(negative, 7)).astype(BF16)
    row = lax.broadcasted_iota(jnp.int32, (low, negative.shape[1]), 0)
    hot_low = flag(row == (negative & (low - 1))).astype(BF16)
    grid = mxu(hot_high, hot_low, LANES)
    times_ref[...] = jnp.concatenate([grid[i : i + 1] for i in range(high)], axis=1)

    height, width = table_ref.shape
    full_ref[...] = near_ref[...]

    @pl.when(crossed_ref[0] == 1)
    def _():
        for start, piece in zip(starts, joined):
            copy = pltpu.make_async_copy(piece, full_ref.at[start : start + piece.shape[0]], done)
            copy.start()
            copy.wait()

    table = full_ref[:height]
    table_ref[...] = table
    for place, part in enumerate(parts_of(table, 3)):
        parts_ref[place] = part
    rows = [full_ref[row : row + 1] for row in range(height, height + height // width)]
    state_ref[...] = jnp.concatenate(rows, axis=1)


def join(crossed, near, ids, dest, negative, joined, starts, height, devices, own):
    edges = ids.shape[1]
    return pl.pallas_call(
        functools.partial(join_kernel, own, devices, SLOTS, BACK_SLOTS, tuple(starts)),
        out_shape=(
            jax.ShapeDtypeStruct((height, near.shape[1]), F32),
            jax.ShapeDtypeStruct((1, height), F32),
            jax.ShapeDtypeStruct((3, height, near.shape[1]), BF16),
            jax.ShapeDtypeStruct((1, height), F32),
            jax.ShapeDtypeStruct((8, edges), F32),
        ),
        in_specs=[SMEM] + [VMEM] * 4 + [pl.BlockSpec(memory_space=pl.ANY)] * len(joined),
        out_specs=(VMEM,) * 5,
        scratch_shapes=[pltpu.VMEM(near.shape, F32), pltpu.SemaphoreType.DMA],
        compiler_params=pltpu.CompilerParams(vmem_limit_bytes=8 << 20),
        name="join",
    )(crossed, near, ids, dest, negative, *joined)


def edge_kernel(
    count_ref, got_ref, parts_ref, times_ref, place_ref, loss_ref, back_ref, source_ref, weight_ref
):
    across = lax.broadcasted_iota(jnp.int32, (source_ref.shape[0], got_ref.shape[0]), 1).astype(F32)
    got_hot = flag(across == to_column(place_ref[0:1])).astype(BF16)
    source = pick(got_hot, parts_of(got_ref[...], 3))
    source_ref[...] = source
    table = [parts_ref[part] for part in range(3)]
    scores = product(parts_of(source, 3), table, LANES)
    edges, height = scores.shape
    times = times_ref[...]
    across = lax.broadcasted_iota(jnp.int32, (edges, height), 1).astype(F32)
    hot = across == to_column(place_ref[2:3])
    positive = jnp.sum(jnp.where(hot, scores, 0.0), axis=1, keepdims=True)
    seen = times > 0.0
    top = jnp.max(jnp.where(seen, scores, -jnp.inf), axis=1, keepdims=True)
    top = jnp.maximum(top, positive)
    power = jnp.where(seen, jnp.exp(scores - top), 0.0) * times
    power_positive = jnp.exp(positive - top)
    total = power_positive + jnp.sum(power, axis=1, keepdims=True)
    logsum = top + jnp.log(total)
    edge = lax.broadcasted_iota(jnp.int32, (edges, 1), 0)
    live = flag(edge < count_ref[0, 0])
    loss = live * (logsum - positive)
    loss_ref[...] = jnp.transpose(jnp.broadcast_to(loss, (edges, 128)))[0:1]
    scale = live / total
    dpos = live * (jnp.exp(positive - logsum) - 1.0)
    weight = power * scale + jnp.where(hot, dpos, 0.0)
    weight_ref[...] = weight

    grad = product(parts_of(weight, 2), table)
    down = lax.broadcasted_iota(jnp.int32, (back_ref.shape[0], edges), 0).astype(F32)
    back_hot = flag(down == place_ref[1:2]).astype(BF16)
    back_ref[...] = pick(back_hot, parts_of(grad, 2))


def edge_step(count, got, parts, times, place, devices):
    edges = place.shape[1]
    height, width = parts.shape[1:]
    return pl.pallas_call(
        edge_kernel,
        out_shape=(
            jax.ShapeDtypeStruct((1, edges), F32),
            jax.ShapeDtypeStruct((devices * BACK_SLOTS, width), F32),
            jax.ShapeDtypeStruct((edges, width), F32),
            jax.ShapeDtypeStruct((edges, height), F32),
        ),
        in_specs=[SMEM] + [VMEM] * 4,
        out_specs=(VMEM,) * 4,
        compiler_params=pltpu.CompilerParams(vmem_limit_bytes=8 << 20),
        name="edge_step",
    )(count, got, parts, times, place)


def row_of(column):
    return jnp.transpose(jnp.broadcast_to(column, (column.shape[0], 128)))[0:1]


def column_of(row):
    return jnp.transpose(jnp.broadcast_to(row, (128, row.shape[1])))[:, 0:1]


def adagrad_rows(emb, state, grad):
    state_new = column_of(state) + jnp.mean(grad * grad, axis=1, keepdims=True)
    emb_new = emb - grad * (0.1 / (jnp.sqrt(state_new) + 1e-10))
    return emb_new, row_of(state_new)


def table_kernel(
    own, slots, back_slots, first_ref, weight_ref, source_ref, table_ref, state_ref, ids_ref, rows_ref,
    new_ref, state_new_ref, used_ref, local_ref, held_ref,
):
    held_ref[...] = rows_ref[...]
    ids = ids_ref[...]
    devices = ids.shape[0]
    most = jnp.zeros((devices, 1), F32)
    for chip in range(devices // 2):
        counts = []
        for device in (2 * chip, 2 * chip + 1):
            mine = flag((ids >= device * own) & (ids < (device + 1) * own))
            counts.append(jnp.sum(mine, axis=1, keepdims=True))
            most = jnp.maximum(most, counts[-1] - back_slots)
        most = jnp.maximum(most, counts[0] + counts[1] - slots)
    used_ref[...] = jnp.max(most, axis=0, keepdims=True)
    local = ids - first_ref[0]
    rank = rank_of(flag((local >= 0) & (local < own)))
    row = row_of(slot_column(rank, local.astype(F32) + 1.0, back_slots))
    down = lax.broadcasted_iota(jnp.int32, local_ref.shape, 0).astype(F32)
    local_ref[...] = flag(down == row).astype(BF16)
    grad = product(parts_of(weight_ref[...], 2), parts_of(source_ref[...], 2), FIRST)
    new_ref[...], state_new_ref[...] = adagrad_rows(table_ref[...], state_ref[...], grad)


def table_step(place, weight, source, table, state, ids, rows):
    own = rows.shape[0]
    return pl.pallas_call(
        functools.partial(table_kernel, own, SLOTS, BACK_SLOTS),
        out_shape=(
            jax.ShapeDtypeStruct(table.shape, F32),
            jax.ShapeDtypeStruct(state.shape, F32),
            jax.ShapeDtypeStruct((1, 1), F32),
            jax.ShapeDtypeStruct((own, ids.shape[0] * BACK_SLOTS), BF16),
            jax.ShapeDtypeStruct(rows.shape, F32),
        ),
        in_specs=[SMEM] + [VMEM] * 6,
        out_specs=(VMEM,) * 5,
        compiler_params=pltpu.CompilerParams(vmem_limit_bytes=8 << 20),
        name="table_step",
    )(place, weight, source, table, state, ids, rows)


def source_kernel(local_ref, back_ref, rows_ref, state_ref, new_ref, state_new_ref):
    grad = pick(local_ref[...], parts_of(back_ref[...], 2))
    new_ref[...], state_new_ref[...] = adagrad_rows(rows_ref[...], state_ref[...], grad)


def source_step(local, back, rows, state):
    return pl.pallas_call(
        source_kernel,
        out_shape=(
            jax.ShapeDtypeStruct(rows.shape, F32),
            jax.ShapeDtypeStruct(state.shape, F32),
        ),
        in_specs=[VMEM] * 4,
        out_specs=(VMEM, VMEM),
        compiler_params=pltpu.CompilerParams(vmem_limit_bytes=4 << 20),
        name="source_step",
    )(local, back, rows, state)


def exact(left, right, dims=ROWS):
    return lax.dot_general(left, right, dims, precision=lax.Precision.HIGHEST, preferred_element_type=F32)


def held_kernel(rows_ref, table_ref, rows_out, table_out):
    rows_out[...] = rows_ref[...]
    table_out[...] = table_ref[...]


def held(rows, table):
    return pl.pallas_call(
        held_kernel,
        out_shape=(jax.ShapeDtypeStruct(rows.shape, F32), jax.ShapeDtypeStruct(table.shape, F32)),
        in_specs=[VMEM] * 2,
        out_specs=(VMEM, VMEM),
        compiler_params=pltpu.CompilerParams(vmem_limit_bytes=4 << 20),
        name="held",
    )(rows, table)


def update_kernel(emb_ref, state_ref, grad_ref, new_ref, state_new_ref):
    new_ref[...], state_new_ref[...] = adagrad_rows(emb_ref[...], state_ref[...], grad_ref[...])


def update(emb, state, grad):
    return pl.pallas_call(
        update_kernel,
        out_shape=(jax.ShapeDtypeStruct(emb.shape, F32), jax.ShapeDtypeStruct(state.shape, F32)),
        in_specs=[VMEM] * 3,
        out_specs=(VMEM, VMEM),
        compiler_params=pltpu.CompilerParams(vmem_limit_bytes=6 << 20),
        name="update",
    )(emb, state, grad)


def everywhere(value):
    copies = jnp.broadcast_to(value, (lax.axis_size(SRC),) + value.shape)
    return lax.all_to_all(copies, SRC, 0, 0, tiled=True).reshape(-1, value.shape[-1])


def whole_step(rows, rows_state, table, table_state, ids, all_ids, dest, negative, count, first):
    rows, table = held(rows, table)
    piece = everywhere(rows)
    columns = jnp.arange(piece.shape[0], dtype=jnp.int32)
    sources = exact((ids[:, None] == columns[None, :]).astype(F32), piece)
    index = jnp.arange(table.shape[0], dtype=jnp.int32)
    hot_dest = (dest[:, None] == index[None, :]).astype(F32)
    hot_negative = (negative[:, None] == index[None, :]).astype(F32)
    targets = exact(hot_dest, table)
    negatives = exact(hot_negative, table)
    positive = jnp.sum(sources * targets, axis=1)
    scores = exact(sources, negatives, LANES)
    live = (jnp.arange(ids.shape[0], dtype=jnp.int32) < count).astype(F32)
    top = jnp.maximum(jnp.max(scores, axis=1), positive)
    total = jnp.exp(positive - top) + jnp.sum(jnp.exp(scores - top[:, None]), axis=1)
    logsum = top + jnp.log(total)
    loss = live * (logsum - positive)
    dpos = live * (jnp.exp(positive - logsum) - 1.0)
    dneg = live[:, None] * jnp.exp(scores - logsum[:, None])
    source_grad = dpos[:, None] * targets + exact(dneg, negatives)
    dest_grad = exact(hot_dest, dpos[:, None] * sources, FIRST)
    dest_grad = dest_grad + exact(hot_negative, exact(dneg, sources, FIRST), FIRST)
    grad_piece = everywhere(source_grad)
    own_index = first + jnp.arange(rows.shape[0], dtype=jnp.int32)
    onehot = (all_ids.reshape(-1)[:, None] == own_index[None, :]).astype(F32)
    own_grad = exact(onehot, grad_piece, FIRST)
    return update(rows, rows_state, own_grad) + update(table, table_state, dest_grad) + (loss[None],)


def after(value, *others):
    return lax.optimization_barrier((value,) + others)[0]


def permute(value, axes, pairs):
    return lax.ppermute(value, axes, pairs)


def with_state_kernel(table_ref, state_ref, full_ref):
    height, width = table_ref.shape
    full_ref[:height] = table_ref[...]
    for row in range(height // width):
        full_ref[height + row : height + row + 1] = state_ref[:, row * width : (row + 1) * width]
    full_ref[height + height // width :] = jnp.zeros((full_ref.shape[0] - height - height // width, width), F32)


def with_state(table, state):
    height, width = table.shape
    return pl.pallas_call(
        with_state_kernel,
        out_shape=jax.ShapeDtypeStruct((height + -(-height // (8 * width)) * 8, width), F32),
        in_specs=[VMEM] * 2,
        out_specs=VMEM,
        compiler_params=pltpu.CompilerParams(vmem_limit_bytes=4 << 20),
        name="with_state",
    )(table, state)


def shifted(table, state):
    wide, deep = lax.axis_size("x"), lax.axis_size("y")
    plane = wide * deep
    count = len(LEAVE)
    full = with_state(table, state)
    size = -(-full.shape[0] // (8 * count)) * 8
    rest = full.shape[0] - size
    starts = [rest] + [min(size * piece, rest - size) for piece in range(count - 1)]
    spot = lambda at: (at[0] % wide) * deep + at[1] % deep
    leave, land = [spot(at) for at in LEAVE], [spot(at) for at in LAND]
    spread = [
        permute(table[starts[k] : starts[k] + size], ("x", "y"), [(leave[0], leave[k])]) for k in range(1, count)
    ]
    at = lax.axis_index("x") * deep + lax.axis_index("y")
    going = jnp.where(at == leave[0], full[starts[0] :], sum(spread))
    near = permute(after(full, *spread), DST, [(j, j + 1) for j in range(2 * plane - 1) if j != plane - 1])
    come = permute(
        going,
        DST,
        [(z * plane + leave[k], (1 - z) * plane + land[k]) for z in range(2) for k in range(count)],
    )
    joined = [come] + [permute(come, ("x", "y"), [(land[k], land[0])]) for k in range(1, count)]
    return near, joined, starts, (at == land[0]).astype(jnp.int32), spread[0]


def on_device(src_emb, src_state, dst_emb, dst_state, src_ids, dst_ids, neg_ids, counts):
    devices = lax.axis_size(SRC)
    rows, rows_state = src_emb[0, 0], src_state[0]
    own = rows.shape[0]
    core = lax.axis_index("core")
    first = lax.axis_index(SRC) * own
    place = jnp.stack([first, first + own * (1 - 2 * core), core])
    ids = src_ids[0]
    edge = lax.broadcasted_iota(jnp.int32, ids.shape, 1)
    ids = jnp.where(edge < counts[0, 0], ids, -1)
    near, joined, starts, crossed, spread = shifted(dst_emb[0, 0], dst_state[0])
    other = permute(after(rows, spread), "core", [(0, 1), (1, 0)])
    all_ids = lax.all_to_all(jnp.broadcast_to(ids, (devices, ids.shape[1])), SRC, 0, 0, tiled=True)

    send = pack_rows(place, all_ids, rows, other, SLOTS)
    got = lax.all_to_all(after(send, near, joined[0]), "zl", 0, 0, tiled=True)
    table, table_state, *prepared = join(
        crossed.reshape(1), near, ids, dst_ids[0], neg_ids[0], joined, starts, dst_emb.shape[2], devices, own
    )
    loss, back, source, weight = edge_step(counts, got, *prepared, devices)
    back = lax.all_to_all(back, SRC, 0, 0, tiled=True)
    dst_new, dst_state_new, over, local, kept = table_step(place, weight, source, table, table_state, all_ids, rows)
    src_new, src_state_new = source_step(local, back, kept, rows_state)

    def again(carry):
        found = whole_step(
            rows, rows_state, table, table_state, ids[0], all_ids, dst_ids[0, 0], neg_ids[0, 0], counts[0, 0], first
        )
        return (jnp.float32(0.0),) + found

    fast = (over[0, 0], src_new, src_state_new, dst_new, dst_state_new, loss)
    done = lax.while_loop(lambda carry: carry[0] > 0.0, again, fast)
    src_new, src_state_new, dst_new, dst_state_new, loss = done[1:]
    return src_new[None, None], src_state_new[None], dst_new[None, None], dst_state_new[None], loss[None]


def solution(mesh):
    sources, dests = mesh.devices.shape
    side = math.isqrt(dests // 2)
    mesh = Mesh(mesh.devices.reshape(sources // 2, 2, 2, side, side), SRC + DST)
    spec = lambda rank: P(SRC, DST, *([None] * (rank - 2)))
    return jax.shard_map(
        on_device,
        mesh=mesh,
        in_specs=tuple(spec(rank) for rank in (4, 3, 4, 3, 3, 3, 3, 2)),
        out_specs=tuple(spec(rank) for rank in (4, 3, 4, 3, 3)),
        check_vma=False,
    )
```
